256 devices in a mesh: ctx: 16 (over z_hi, x), exp: 8 (over y, z_lo), dp: 2 (over core).
Axes of the slice: x: 4, y: 4, z: 8 (z_hi: 4, z_lo: 2; z = z_hi * 2 + z_lo), core: 2. Of those that a mesh axis runs over, the one named last changes fastest.
Arguments:
- query: bfloat16 [2, 2048, 10240], P('dp', 'ctx', 'exp'), may hold values from -6 to 6
- key_rows: bfloat16 [2, 4096, 1024], P('dp', 'ctx', 'exp'), may hold values from -6 to 6
- value_rows: bfloat16 [2, 4096, 1024], P('dp', 'ctx', 'exp'), may hold values from -6 to 6
- out_grad: bfloat16 [2, 2048, 10240], P('dp', 'ctx', 'exp'), may hold values from -6 to 6
- block_offsets: int32 [16], replicated, may hold values from 0 to 15, each once
- tok_grad: bfloat16 [32768, 6400], P(('ctx', 'exp', 'dp')), may hold values from -0.75 to 0.75
- hidden_act: bfloat16 [32768, 640], P(('ctx', 'exp', 'dp')), may hold values from -6 to 6
- router_prob: bfloat16 [32768], P(('ctx', 'exp', 'dp')), may hold values from 0.19921875 to 1
- expert_ids: int32 [32768, 1], P(('ctx', 'exp', 'dp')), may hold values from 0 to 7; in each aligned block of 128 rows (0 to 127, 128 to 255, ...) at most 24 rows name the same one
- down_weight: bfloat16 [8, 6400, 640], P('exp', ('ctx', 'dp')), may hold values from -0.25 to 0.25
Outputs:
- query_grad: bfloat16 [2, 2048, 10240], P('dp', 'ctx', 'exp')
- key_grad: bfloat16 [2, 4096, 1024], P('dp', 'ctx', 'exp')
- value_grad: bfloat16 [2, 4096, 1024], P('dp', 'ctx', 'exp')
- hidden_grad: bfloat16 [32768, 640], P(('ctx', 'exp', 'dp'))
- route_grad: bfloat16 [32768], P(('ctx', 'exp', 'dp'))
- weight_grad: bfloat16 [8, 6400, 640], P('exp', ('ctx', 'dp'))
The draws below stay inside these ranges and needn't reach their ends.
Inputs may be any that keep to these rules, and one draw needn't show every extreme that they name: `expert_ids`: within the 128 rows of one device no expert is named by more than 24 rows. `block_offsets`: each block number appears once.
All inputs are finite; a program needn't handle non-finite values.
Results may differ from the reference program's by a relative error of at most 0.025.
Values may be sent and summed in bfloat16 or wider, within the bound.
A program may use at most 128 MiB of HBM per device.

```python
import math
import jax
import jax.numpy as jnp
import numpy as np
from jax import lax

D = 6400
HD = 128
GROUP = 10
FF = 640
KEY_DEV = 256
TOK_DEV = 128
QRY_DEV = 128
KV_HEADS = 8
Q_HEADS = 80
SEQS = 2
WINDOW = 4096
QUERIES = 2048
EXPERTS = 8
CAP = 24
TOKENS = 32768
N_CTX = 16
N_EXP = 8
N_DP = 2


def draw_query(key, part):
    key = jax.random.fold_in(key, 3)
    full_shape = (SEQS, QUERIES, Q_HEADS * HD)
    return jnp.clip(jax.random.normal(key, full_shape, jnp.float32), -6.0, 6.0).astype(jnp.bfloat16)


def draw_key_rows(key, part):
    key = jax.random.fold_in(key, 5)
    full_shape = (SEQS, WINDOW, KV_HEADS * HD)
    return jnp.clip(jax.random.normal(key, full_shape, jnp.float32), -6.0, 6.0).astype(jnp.bfloat16)


def block_levels(stream_key, dims, cuts, smallest, high):
    gain = 1.0
    for dim, parts in cuts:
        heights = jax.random.uniform(jax.random.fold_in(jax.random.fold_in(stream_key, 6), dim), (parts,), jnp.float32, smallest / len(cuts), high / len(cuts))
        gain = gain * jnp.repeat(jnp.exp(heights), dims[dim] // parts).reshape((-1,) + (1,) * (len(dims) - 1 - dim))
    return gain


def deal_out(rng, own, number, rows, count, top, bound, slope):
    sequence = jax.random.permutation(rng, count)
    crowded, usual = shares(count, rows * top, bound, slope, True), shares(count, rows * top, bound, slope, False)
    places = jnp.arange(count)

    def named(lengths, turn):
        used = int((lengths > 0).sum())
        fixed = max(1, used // 4)
        passed = fixed + (places - fixed + turn * (used - fixed)) % max(1, count - fixed)
        return jnp.zeros((count,), jnp.int32).at[sequence[jnp.where(places < fixed, places, passed)]].set(jnp.asarray(lengths, jnp.int32))

    lengths = jnp.where(number % 4 == 0, named(crowded, number // 4), named(usual, number - number // 4 - 1))
    mixed = jax.random.permutation(jax.random.fold_in(own, 3), count)
    source_of, receiver = mixed[0:count // 2 * 2:2], mixed[1:count // 2 * 2:2]
    slack = jnp.minimum(lengths[source_of] - 1, bound - lengths[receiver]) // 2
    slack = jnp.where((source_of == sequence[0]) | (receiver == sequence[0]) | (lengths[receiver] == 0), 0, jnp.maximum(slack, 0))
    passed = jax.random.randint(jax.random.fold_in(own, 4), (count // 2,), 0, 1 << 20) % (slack + 1)
    lengths = lengths.at[source_of].add(-passed).at[receiver].add(passed)
    members = jnp.searchsorted(jnp.cumsum(lengths), jnp.arange(rows * top), side="right").astype(jnp.int32)
    table = members.reshape(top, rows).T
    table = table[jax.random.permutation(jax.random.fold_in(own, 1), rows)]
    turn = jax.random.randint(jax.random.fold_in(own, 2), (rows, 1), 0, top)
    return jnp.take_along_axis(table, (jnp.arange(top)[None, :] + turn) % top, axis=1)


def shares(count, total, reach, slope, full):
    weights = [(1 << 20) // math.isqrt(standing ** slope) + 1 for standing in range(1, count + 1)]
    largest = reach if full else min(reach, max(-(-total // count), total * weights[0] // sum(weights)))
    least = 1 if total - largest >= count - 1 else 0
    given, rest = [largest] + [least] * (count - 1), total - largest - least * (count - 1)
    while rest > 0:
        movable = [i for i in range(1, count) if given[i] < largest] or [i for i in range(1, count) if given[i] < reach]
        whole, remaining = sum([weights[i] for i in movable]), rest
        for i in movable:
            more = min(reach - given[i], max(1, remaining * weights[i] // whole), rest)
            given[i] = given[i] + more
            rest = rest - more
    return np.array(given)


def scatter_about(own_key, shape, spread, most, shards=(), held_as=jnp.bfloat16):
    values = spread * jax.random.normal(own_key, shape, jnp.float32)
    if shards:
        values = values * block_levels(own_key, shape, shards, -0.22, 0.18)
    return jnp.clip(values, -most, most).astype(held_as)


def setup_inputs(seed: int = 0) -> dict:
    seeds = jax.random.split(jax.random.key(seed), 11)
    query = draw_query(jax.random.fold_in(seeds[10], 71), 0)
    key_rows = draw_key_rows(jax.random.fold_in(seeds[10], 71), 0)
    value_rows = scatter_about(seeds[2], (SEQS, WINDOW, KV_HEADS * HD), 1.0, 6.0, ((0, 2), (1, 16), (2, 8)))
    out_grad = scatter_about(seeds[3], (SEQS, QUERIES, Q_HEADS * HD), 1.0, 6.0, ((0, 2), (1, 16), (2, 8)))
    block_offsets = jax.random.permutation(seeds[4], N_CTX).astype(jnp.int32)
    tok_grad = scatter_about(seeds[5], (TOKENS, D), 0.125, 0.75, ((0, 256),))
    hidden_act = scatter_about(seeds[6], (TOKENS, FF), 1.0, 6.0, ((0, 256),))
    router_prob = jnp.clip(0.19921875 + 0.80078125 * jax.random.uniform(seeds[7], (TOKENS,), jnp.float32) ** block_levels(seeds[7], (TOKENS,), ((0, 256),), -0.2, 0.2), 0.19921875, 1.0).astype(jnp.bfloat16)
    expert_ids_keys = jax.random.split(jax.random.fold_in(seeds[8], 1), TOKENS // TOK_DEV)
    expert_ids_turns = jax.random.permutation(jax.random.fold_in(seeds[8], 3), TOKENS // TOK_DEV)
    expert_ids = jax.vmap(lambda own, number: deal_out(jax.random.fold_in(seeds[8], 2), own, number, TOK_DEV, EXPERTS, 1, CAP, 1))(expert_ids_keys, expert_ids_turns).reshape((TOKENS, 1))
    down_weight = scatter_about(seeds[9], (EXPERTS, D, FF), FF ** -0.5, 0.25, ((0, 8), (1, 32)))
    return {"query": query, "key_rows": key_rows, "value_rows": value_rows, "out_grad": out_grad, "block_offsets": block_offsets, "tok_grad": tok_grad, "hidden_act": hidden_act, "router_prob": router_prob, "expert_ids": expert_ids, "down_weight": down_weight}


def head_backward(query_head, grad_head, key_head, value_head, visible, inv_root):
    scores = jnp.dot(query_head, key_head.T, preferred_element_type=jnp.float32) * inv_root
    row_peak = lax.optimization_barrier(jnp.max(jnp.where(visible, scores, -jnp.inf), axis=1, keepdims=True))
    unnormed = jnp.where(visible, jnp.exp(jnp.where(visible, scores - row_peak, 0.0)), 0.0)
    softmaxed = unnormed / lax.optimization_barrier(jnp.sum(unnormed, axis=1, keepdims=True))
    attn_out = jnp.dot(softmaxed, value_head.astype(jnp.float32), precision=lax.Precision.HIGHEST)
    row_delta = lax.optimization_barrier(jnp.sum(grad_head.astype(jnp.float32) * attn_out, axis=1, keepdims=True))
    probs_low = softmaxed.astype(jnp.bfloat16)
    value_part = jnp.dot(probs_low.T, grad_head, preferred_element_type=jnp.float32)
    prob_grad = jnp.dot(grad_head, value_head.T, preferred_element_type=jnp.float32)
    score_grad = (softmaxed * (prob_grad - row_delta)).astype(jnp.bfloat16)
    query_part = jnp.dot(score_grad, key_head, preferred_element_type=jnp.float32) * inv_root
    key_part = jnp.dot(score_grad.T, query_head, preferred_element_type=jnp.float32) * inv_root
    return (query_part, key_part, value_part)

def attention_backward(query, key_rows, value_rows, out_grad, block_offsets):
    inv_root = 1.0 / math.sqrt(HD)
    query_index = jnp.arange(QUERIES)
    query_pos = block_offsets[query_index // QRY_DEV] * KEY_DEV + (KEY_DEV - QRY_DEV) + query_index % QRY_DEV
    key_index = jnp.arange(WINDOW)
    key_pos = block_offsets[key_index // KEY_DEV] * KEY_DEV + key_index % KEY_DEV
    visible = key_pos[None, :] <= query_pos[:, None]
    query_list, key_list, value_list = ([], [], [])
    for seq_index in range(SEQS):
        query_heads = query[seq_index].reshape(QUERIES, KV_HEADS, GROUP, HD).transpose(1, 2, 0, 3)
        grad_heads = out_grad[seq_index].reshape(QUERIES, KV_HEADS, GROUP, HD).transpose(1, 2, 0, 3)
        key_heads = key_rows[seq_index].reshape(WINDOW, KV_HEADS, HD).transpose(1, 0, 2)
        value_heads = value_rows[seq_index].reshape(WINDOW, KV_HEADS, HD).transpose(1, 0, 2)

        def group_backward(operands):
            group_queries, group_grads, key_head, value_head = operands

            def one_head(running, pair):
                query_part, key_part, value_part = head_backward(pair[0], pair[1], key_head, value_head, visible, inv_root)
                return ((running[0] + key_part, running[1] + value_part), query_part)
            zero_rows = jnp.zeros((WINDOW, HD), jnp.float32)
            sums, query_parts = lax.scan(one_head, (zero_rows, zero_rows), (group_queries, group_grads))
            return (query_parts, sums[0], sums[1])
        query_parts, key_sums, value_sums = lax.map(group_backward, (query_heads, grad_heads, key_heads, value_heads))
        query_list.append(query_parts.transpose(2, 0, 1, 3).reshape(QUERIES, Q_HEADS * HD).astype(jnp.bfloat16))
        key_list.append(key_sums.transpose(1, 0, 2).reshape(WINDOW, KV_HEADS * HD).astype(jnp.bfloat16))
        value_list.append(value_sums.transpose(1, 0, 2).reshape(WINDOW, KV_HEADS * HD).astype(jnp.bfloat16))
    return (jnp.stack(query_list), jnp.stack(key_list), jnp.stack(value_list))

def expert_backward(tok_grad, hidden_act, router_prob, expert_ids, down_weight):
    group_total = N_CTX * N_DP
    bucket_len = N_EXP * CAP
    route_ids = expert_ids[:, 0].astype(jnp.int32)
    device_block = jnp.arange(TOKENS, dtype=jnp.int32) // TOK_DEV
    group_index = device_block // (N_EXP * N_DP) * N_DP + device_block % N_DP
    bucket_code = route_ids * group_total + group_index
    sort_order = jnp.argsort(bucket_code, stable=True).astype(jnp.int32)
    counts = jax.ops.segment_sum(jnp.ones((TOKENS,), jnp.int32), bucket_code, num_segments=EXPERTS * group_total)
    starts = jnp.cumsum(counts) - counts
    sorted_code = bucket_code[sort_order]
    rank = jnp.arange(TOKENS, dtype=jnp.int32) - starts[sorted_code]
    slot_table = jnp.full((EXPERTS * group_total * bucket_len,), TOKENS, jnp.int32)
    slot_table = slot_table.at[sorted_code * bucket_len + rank].set(sort_order).reshape(EXPERTS, group_total * bucket_len)
    grad_pad = jnp.concatenate([tok_grad, jnp.zeros((1, D), tok_grad.dtype)], axis=0)
    act_pad = jnp.concatenate([hidden_act, jnp.zeros((1, FF), hidden_act.dtype)], axis=0)
    prob_pad = jnp.concatenate([router_prob.astype(jnp.float32), jnp.zeros((1,), jnp.float32)], axis=0)

    def per_expert(operands):
        index_row, weight = operands
        grad_rows = grad_pad[index_row]
        act_rows = act_pad[index_row]
        prob_rows = prob_pad[index_row]
        hidden_part = prob_rows[:, None] * jnp.dot(grad_rows, weight, preferred_element_type=jnp.float32)
        expert_out = jnp.dot(act_rows, weight.T, preferred_element_type=jnp.float32)
        route_part = lax.optimization_barrier(jnp.sum(grad_rows.astype(jnp.float32) * expert_out, axis=1))
        scaled_grad = (prob_rows[:, None] * grad_rows.astype(jnp.float32)).astype(jnp.bfloat16)

        def add_group(running, pair):
            partial_value = jnp.dot(pair[0].T, pair[1], preferred_element_type=jnp.float32).astype(jnp.bfloat16)
            partial_value = lax.optimization_barrier(partial_value)
            return (running + partial_value.astype(jnp.float32), None)
        weight_sum, _ = lax.scan(add_group, jnp.zeros((D, FF), jnp.float32), (scaled_grad.reshape(group_total, bucket_len, D), act_rows.reshape(group_total, bucket_len, FF)))
        return (hidden_part.astype(jnp.bfloat16), route_part.astype(jnp.bfloat16), weight_sum.astype(jnp.bfloat16))
    hidden_parts, route_parts, weight_grad = lax.map(per_expert, (slot_table, down_weight))
    flat_index = slot_table.reshape(-1)
    hidden_grad = jnp.zeros((TOKENS + 1, FF), jnp.bfloat16).at[flat_index].set(hidden_parts.reshape(-1, FF))[:TOKENS]
    route_grad = jnp.zeros((TOKENS + 1,), jnp.bfloat16).at[flat_index].set(route_parts.reshape(-1))[:TOKENS]
    return (hidden_grad, route_grad, weight_grad)

def reference(query, key_rows, value_rows, out_grad, block_offsets, tok_grad, hidden_act, router_prob, expert_ids, down_weight):
    query_grad, key_grad, value_grad = attention_backward(query, key_rows, value_rows, out_grad, block_offsets)
    hidden_grad, route_grad, weight_grad = expert_backward(tok_grad, hidden_act, router_prob, expert_ids, down_weight)
    return (query_grad, key_grad, value_grad, hidden_grad, route_grad, weight_grad)
```

```python
import math

import jax
import jax.numpy as jnp
from jax import lax
from jax.experimental import pallas as pl
from jax.experimental.pallas import tpu as pltpu
from jax.sharding import PartitionSpec as P

HD = 128
GROUP = 10
NEG_FILL = -1e30
MESH = pl.DeviceIdType.MESH
F32 = jnp.float32
BF16 = jnp.bfloat16

NX, NZ, NE, ND = 4, 4, 8, 2
KEYS = 256
QRY = 128
COLS = GROUP * QRY
TOK = 128
CAP = 24
D = 6400
HALF = D // 2
FF = 640
PART = (HALF + FF) // 2
WB = 400
WS = 200
WP = 208
SLOTS = NE * CAP
ROWS = ND * SLOTS

NT = (((1,), (1,)), ((), ()))
TN = (((0,), (0,)), ((), ()))


def dot(a, b, dims=(((1,), (0,)), ((), ()))):
    return lax.dot_general(a, b, dims, preferred_element_type=F32)


def kernel(
    off_ref,
    q_ref,
    k_ref,
    v_ref,
    do_ref,
    tok_ref,
    act_ref,
    prob_ref,
    idr_ref,
    idc_ref,
    w_ref,
    dq_out,
    dk_out,
    dv_out,
    hid_out,
    route_out,
    dw_out,
    kv,
    qs,
    dos,
    stat_m,
    stat_l,
    stat_d,
    p_buf,
    ds_buf,
    dq_acc,
    dkv,
    dkv_x,
    dkv_zs,
    dkv_zr,
    perm,
    tsend,
    trecv,
    gbuf,
    abuf,
    wpad,
    wraw,
    wfull,
    wg,
    wg_x,
    wg_zs,
    wg_zr,
    hsend,
    hrecv,
    kz_s,
    kz_r,
    kx_s,
    kx_r,
    wz_s,
    wz_r,
    wx_s,
    wx_r,
    tk_s,
    tk_r,
    dx_s,
    dx_r,
    dz_s,
    dz_r,
    gx_s,
    gx_r,
    gz_s,
    gz_r,
    hb_s,
    hb_r,
):
    ctx = lax.axis_index("ctx")
    exp = lax.axis_index("exp")
    core = lax.axis_index("dp")
    z = ctx // NX
    x = ctx % NX
    inv_root = 1.0 / math.sqrt(HD)
    scale2 = inv_root * math.log2(math.e)

    def xpeer(dx):
        return lax.rem(x + dx, NX)

    def zpeer(dz):
        return lax.rem(z + dz, NZ)

    def remote(src, dst, ss, rs, dev):
        return pltpu.make_async_remote_copy(
            src_ref=src, dst_ref=dst, send_sem=ss, recv_sem=rs, device_id=dev, device_id_type=MESH
        )

    barrier = pltpu.get_barrier_semaphore()
    count = 0
    for dx in range(1, NX):
        pl.semaphore_signal(
            barrier, inc=1, device_id=(z * NX + xpeer(dx), exp, core), device_id_type=MESH
        )
        count += 1
    for dz in range(0, NZ):
        for dh in range(ND):
            if dz == 0 and dh == 0:
                continue
            pl.semaphore_signal(
                barrier,
                inc=1,
                device_id=(zpeer(dz) * NX + x, exp, lax.rem(core + dh, ND)),
                device_id_type=MESH,
            )
            count += 1
    for de in range(1, NE):
        for dh in range(ND):
            pl.semaphore_signal(
                barrier,
                inc=1,
                device_id=(ctx, lax.rem(exp + de, NE), lax.rem(core + dh, ND)),
                device_id_type=MESH,
            )
            count += 1
    pl.semaphore_wait(barrier, count)

    kv[x, z, 0:KEYS] = k_ref[...]
    kv[x, z, KEYS : 2 * KEYS] = v_ref[...]

    def kz_copy(dz):
        return remote(
            kv.at[x, z],
            kv.at[x, z],
            kz_s.at[dz - 1],
            kz_r.at[dz - 1],
            (zpeer(dz) * NX + x, exp, core),
        )

    def kx_copy(dx, dz):
        zz = zpeer(NZ - dz)
        return remote(
            kv.at[x, zz],
            kv.at[x, zz],
            kx_s.at[(dx - 1) * NZ + dz],
            kx_r.at[(dx - 1) * NZ + dz],
            (z * NX + xpeer(dx), exp, core),
        )

    for dz in range(1, NZ):
        kz_copy(dz).start()
    for dx in range(1, NX):
        kx_copy(dx, 0).start()

    wpad[0:WS] = w_ref[...]
    wpad[WS:WP] = jnp.zeros((WP - WS, FF), BF16)
    w_core = z // 2
    w_slot = lax.rem(z, 2)
    w_here = core == w_core

    def wz_copy(dz):
        return remote(
            wpad,
            wraw.at[w_slot, core],
            wz_s.at[dz],
            wz_r.at[w_slot * 2 + core],
            (zpeer(dz) * NX + x, exp, w_core),
        )

    for dz in range(1, NZ):
        wz_copy(dz).start()

    @pl.when(w_here)
    def _():
        wraw[w_slot, core] = wpad[...]

    @pl.when(jnp.logical_not(w_here))
    def _():
        wz_copy(0).start()

    ids_row = idr_ref[...]
    row_at = lax.broadcasted_iota(jnp.int32, (TOK, TOK), 0)
    col_at = lax.broadcasted_iota(jnp.int32, (TOK, TOK), 1)
    same = jnp.where((idc_ref[...] == ids_row) & (row_at < col_at), 1.0, 0.0)
    rank = jnp.sum(same, axis=0, keepdims=True).astype(jnp.int32)
    target = ids_row * CAP + rank
    slot_at = lax.broadcasted_iota(jnp.int32, (SLOTS, TOK), 0)
    perm[...] = jnp.where(slot_at == target, 1.0, 0.0).astype(BF16)
    scaled_act = (prob_ref[...] * act_ref[...].astype(F32)).astype(BF16)

    def tk_copy(de, dh):
        e_to = lax.rem(exp + de, NE)
        h_to = lax.rem(core + dh, ND)
        i = de * ND + dh
        return remote(
            tsend.at[h_to, e_to],
            trecv.at[core, exp],
            tk_s.at[i],
            tk_r.at[i],
            (ctx, e_to, h_to),
        )

    for half in range(ND):
        base = half * HALF
        first = dot(perm[...], tok_ref[:, base : base + PART])
        second = dot(perm[...], tok_ref[:, base + PART : base + HALF])
        third = dot(perm[...], scaled_act)
        for e in range(NE):
            rows = slice(e * CAP, (e + 1) * CAP)
            tsend[half, e, :, 0 : HALF - PART] = jnp.concatenate(
                [first[rows, 0 : HALF - PART], second[rows]], axis=0
            ).astype(BF16)
            tsend[half, e, :, HALF - PART : PART] = jnp.concatenate(
                [first[rows, HALF - PART : PART], third[rows]], axis=0
            ).astype(BF16)
    for de in range(NE):
        for dh in range(ND):
            if de == 0 and dh == 0:
                trecv[core, exp] = tsend[core, exp]
            else:
                tk_copy(de, dh).start()

    for h in range(GROUP):
        qs[h * QRY : (h + 1) * QRY] = q_ref[:, h * HD : (h + 1) * HD]
        dos[h * QRY : (h + 1) * QRY] = do_ref[:, h * HD : (h + 1) * HD]

    for dz in range(1, NZ):
        kz_copy(dz).wait_recv()
        for dx in range(1, NX):
            kx_copy(dx, dz).start()

    def wx_copy(dx, s):
        at = pl.ds(pl.multiple_of((s * NX + x) * WB, WB), WB)
        return remote(
            wfull.at[at],
            wfull.at[at],
            wx_s.at[(dx - 1) * 2 + s],
            wx_r.at[(dx - 1) * 2 + s],
            (z * NX + xpeer(dx), exp, core),
        )

    for s in range(2):
        for h in range(ND):

            @pl.when(jnp.logical_not((2 * core + s == z) & (core == h)))
            def _():
                remote(
                    wpad, wraw.at[s, h], wz_s.at[0], wz_r.at[s * 2 + h], (ctx, exp, core)
                ).wait_recv()

        merged = jnp.concatenate(
            [wraw[s, 0, 0:WS].astype(F32), wraw[s, 1, 0:WS].astype(F32)], axis=0
        )
        wfull[pl.ds(pl.multiple_of((s * NX + x) * WB, WB), WB)] = merged.astype(BF16)
        for dx in range(1, NX):
            wx_copy(dx, s).start()

    own_pos = off_ref[ctx] * KEYS + (KEYS - QRY)
    q_pos = own_pos + lax.broadcasted_iota(jnp.int32, (KEYS, QRY), 1)
    k_at = lax.broadcasted_iota(jnp.int32, (KEYS, QRY), 0)
    wide = 2 * QRY

    def bias_of(xx, zz):
        seen = off_ref[zz * NX + xx] * KEYS + k_at <= q_pos
        one = jnp.where(seen, 0.0, NEG_FILL)
        return jnp.concatenate([one, one], axis=1)

    stat_m[...] = jnp.full((1, COLS), NEG_FILL, F32)
    stat_l[...] = jnp.zeros((1, COLS), F32)
    stat_d[...] = jnp.zeros((1, COLS), F32)

    def first_pass(xx, zz):
        bias = bias_of(xx, zz)
        keys = kv[xx, zz, 0:KEYS]
        values = kv[xx, zz, KEYS : 2 * KEYS]
        for g in range(COLS // wide):
            at = slice(g * wide, (g + 1) * wide)
            scores = dot(keys, qs[at], NT) * scale2 + bias
            grads = dot(values, dos[at], NT)
            old = stat_m[:, at]
            peak = jnp.maximum(old, jnp.max(scores, axis=0, keepdims=True))
            shrink = jnp.exp2(old - peak)
            probs = jnp.exp2(scores - peak)
            stat_m[:, at] = peak
            stat_l[:, at] = stat_l[:, at] * shrink + jnp.sum(probs, axis=0, keepdims=True)
            stat_d[:, at] = stat_d[:, at] * shrink + jnp.sum(probs * grads, axis=0, keepdims=True)

    for dx in range(NX):
        xx = xpeer(NX - dx)
        if dx:
            for dz in range(NZ):
                zz = zpeer(NZ - dz)
                remote(
                    kv.at[xx, zz],
                    kv.at[xx, zz],
                    kx_s.at[(dx - 1) * NZ + dz],
                    kx_r.at[(dx - 1) * NZ + dz],
                    (ctx, exp, core),
                ).wait_recv()

        @pl.loop(0, NZ)
        def _(zz):
            first_pass(xx, zz)

    total = stat_l[...]
    stat_m[...] = stat_m[...] + jnp.log2(total)
    stat_d[...] = stat_d[...] / total
    dq_acc[...] = jnp.zeros((HD, COLS), F32)

    def second_pass(xx, zz):
        bias = bias_of(xx, zz)
        keys = kv[xx, zz, 0:KEYS]
        values = kv[xx, zz, KEYS : 2 * KEYS]
        for g in range(COLS // wide):
            at = slice(g * wide, (g + 1) * wide)
            scores = dot(keys, qs[at], NT) * scale2 + bias
            grads = dot(values, dos[at], NT)
            probs = jnp.exp2(scores - stat_m[:, at])
            p_buf[:, at] = probs.astype(BF16)
            ds_buf[:, at] = (probs * (grads - stat_d[:, at])).astype(BF16)
        dkv[xx, zz, 0:KEYS] = (dot(ds_buf[...], qs[...]) * inv_root).astype(BF16)
        dkv[xx, zz, KEYS : 2 * KEYS] = dot(p_buf[...], dos[...]).astype(BF16)
        dq_acc[...] += dot(keys, ds_buf[...], TN)

    def dx_copy(dx):
        return remote(
            dkv.at[xpeer(dx)],
            dkv_x.at[dx - 1],
            dx_s.at[dx - 1],
            dx_r.at[dx - 1],
            (z * NX + xpeer(dx), exp, core),
        )

    for dx in (2, 1, 3, 0):
        xx = xpeer(dx)

        @pl.loop(0, NZ)
        def _(zz):
            second_pass(xx, zz)

        if dx:
            dx_copy(dx).start()

    for de in range(NE):
        for dh in range(ND):
            if de or dh:
                tk_copy(de, dh).wait_recv()

    @pl.loop(0, NE)
    def _(i):
        h = i // (NE // 2)
        e = lax.rem(i, NE // 2) * 2
        one = trecv[h, e].astype(F32)
        two = trecv[h, e + 1].astype(F32)
        at = pl.ds(pl.multiple_of(i * 2 * CAP, 2 * CAP), 2 * CAP)
        gbuf[at, 0:PART] = jnp.concatenate([one[0:CAP], two[0:CAP]], axis=0).astype(BF16)
        rest = jnp.concatenate([one[CAP:], two[CAP:]], axis=0).astype(BF16)
        gbuf[at, PART:HALF] = rest[:, 0 : HALF - PART]
        abuf[at] = rest[:, HALF - PART :]

    def gx_copy(dx, s):
        return remote(
            wg.at[pl.ds(pl.multiple_of((s * NX + xpeer(dx)) * WB, WB), WB)],
            wg_x.at[dx - 1, s],
            gx_s.at[(dx - 1) * 2 + s],
            gx_r.at[(dx - 1) * 2 + s],
            (z * NX + xpeer(dx), exp, core),
        )

    for i in range(HALF // FF):
        at = slice(i * FF, (i + 1) * FF)
        wg[at] = dot(gbuf[:, at], abuf[...], TN).astype(BF16)
        if i == 2:
            for dx in range(1, NX):
                gx_copy(dx, 0).start()
    for dx in range(1, NX):
        gx_copy(dx, 1).start()

    for s in range(2):
        for dx in range(1, NX):
            wx_copy(dx, s).wait_recv()
    hidden = dot(gbuf[...], wfull[...])
    for h in range(ND):
        for e in range(NE):
            i = h * NE + e
            hsend[h, e] = hidden[i * CAP : (i + 1) * CAP]

    def hb_copy(de, dh):
        e_to = lax.rem(exp + de, NE)
        h_to = lax.rem(core + dh, ND)
        i = de * ND + dh
        return remote(
            hsend.at[h_to, e_to], hrecv.at[core, exp], hb_s.at[i], hb_r.at[i], (ctx, e_to, h_to)
        )

    for de in range(NE):
        for dh in range(ND):
            if de == 0 and dh == 0:
                hrecv[core, exp] = hsend[core, exp]
            else:
                hb_copy(de, dh).start()

    for h in range(GROUP):
        dq_out[:, h * HD : (h + 1) * HD] = (
            jnp.transpose(dq_acc[:, h * QRY : (h + 1) * QRY]) * inv_root
        ).astype(BF16)

    def dz_copy(dz):
        return remote(
            dkv_zs.at[zpeer(dz)],
            dkv_zr.at[dz - 1],
            dz_s.at[dz - 1],
            dz_r.at[dz - 1],
            (zpeer(dz) * NX + x, exp, core),
        )

    for dx in range(1, NX):
        dx_copy(dx).wait_recv()

    @pl.loop(0, NZ)
    def _(zz):
        sums = dkv[x, zz].astype(F32)
        for i in range(NX - 1):
            sums = sums + dkv_x[i, zz].astype(F32)
        dkv_zs[zz] = sums.astype(BF16)

    for dz in range(1, NZ):
        dz_copy(dz).start()

    def gz_copy(dz, s, h):
        return remote(
            wg_zs.at[s, h],
            wg_zr.at[z],
            gz_s.at[s * 2 + h],
            gz_r.at[z],
            ((2 * core + s) * NX + x, exp, h),
        )

    wg_zs[:, :, WS:WP] = jnp.zeros((2, ND, WP - WS, FF), BF16)
    for s in range(2):
        for dx in range(1, NX):
            gx_copy(dx, s).wait_recv()
        sums = wg[pl.ds(pl.multiple_of((s * NX + x) * WB, WB), WB)].astype(F32)
        for i in range(NX - 1):
            sums = sums + wg_x[i, s].astype(F32)
        for h in range(ND):
            wg_zs[s, h, 0:WS] = sums[h * WS : (h + 1) * WS].astype(BF16)
            own = (2 * core + s == z) & (core == h)

            @pl.when(own)
            def _():
                wg_zr[z] = wg_zs[s, h]

            @pl.when(jnp.logical_not(own))
            def _():
                gz_copy(0, s, h).start()

    for de in range(NE):
        for dh in range(ND):
            if de or dh:
                hb_copy(de, dh).wait_recv()
    back = jnp.concatenate([hrecv[0, e] + hrecv[1, e] for e in range(NE)], axis=0)
    high = back.astype(BF16)
    low = (back - high.astype(F32)).astype(BF16)
    mine = dot(perm[...], high, TN) + dot(perm[...], low, TN)
    hid_out[...] = (prob_ref[...] * mine).astype(BF16)
    route_out[...] = jnp.sum(act_ref[...].astype(F32) * mine, axis=1, keepdims=True).astype(BF16)

    for dz in range(1, NZ):
        dz_copy(dz).wait_recv()
    sums = dkv_zs[z].astype(F32)
    for i in range(NZ - 1):
        sums = sums + dkv_zr[i].astype(F32)
    dk_out[...] = sums[0:KEYS].astype(BF16)
    dv_out[...] = sums[KEYS:].astype(BF16)

    for zz in range(NZ):

        @pl.when(jnp.logical_not((zz == z) & (core == w_core)))
        def _():
            remote(
                wg_zs.at[0, 0], wg_zr.at[zz], gz_s.at[0], gz_r.at[zz], (ctx, exp, core)
            ).wait_recv()

    sums = wg_zr[0].astype(F32)
    for zz in range(1, NZ):
        sums = sums + wg_zr[zz].astype(F32)
    dw_out[...] = sums[0:WS].astype(BF16)

    for dz in range(1, NZ):
        kz_copy(dz).wait_send()
        wz_copy(dz).wait_send()
        dz_copy(dz).wait_send()

    @pl.when(jnp.logical_not(w_here))
    def _():
        wz_copy(0).wait_send()

    for dx in range(1, NX):
        for dz in range(NZ):
            kx_copy(dx, dz).wait_send()
        for s in range(2):
            wx_copy(dx, s).wait_send()
            gx_copy(dx, s).wait_send()
        dx_copy(dx).wait_send()
    for de in range(NE):
        for dh in range(ND):
            if de or dh:
                tk_copy(de, dh).wait_send()
                hb_copy(de, dh).wait_send()
    for s in range(2):
        for h in range(ND):

            @pl.when(jnp.logical_not((2 * core + s == z) & (core == h)))
            def _():
                gz_copy(0, s, h).wait_send()


def per_device(
    query,
    key_rows,
    value_rows,
    out_grad,
    block_offsets,
    tok_grad,
    hidden_act,
    router_prob,
    expert_ids,
    down_weight,
):
    vmem = pl.BlockSpec(memory_space=pltpu.VMEM)
    smem = pl.BlockSpec(memory_space=pltpu.SMEM)
    dma = pltpu.SemaphoreType.DMA
    scratch = [
        pltpu.VMEM((NX, NZ, 2 * KEYS, HD), BF16),
        pltpu.VMEM((COLS, HD), BF16),
        pltpu.VMEM((COLS, HD), BF16),
        pltpu.VMEM((1, COLS), F32),
        pltpu.VMEM((1, COLS), F32),
        pltpu.VMEM((1, COLS), F32),
        pltpu.VMEM((KEYS, COLS), BF16),
        pltpu.VMEM((KEYS, COLS), BF16),
        pltpu.VMEM((HD, COLS), F32),
        pltpu.VMEM((NX, NZ, 2 * KEYS, HD), BF16),
        pltpu.VMEM((NX - 1, NZ, 2 * KEYS, HD), BF16),
        pltpu.VMEM((NZ, 2 * KEYS, HD), BF16),
        pltpu.VMEM((NZ - 1, 2 * KEYS, HD), BF16),
        pltpu.VMEM((SLOTS, TOK), BF16),
        pltpu.VMEM((ND, NE, 2 * CAP, PART), BF16),
        pltpu.VMEM((ND, NE, 2 * CAP, PART), BF16),
        pltpu.VMEM((ROWS, HALF), BF16),
        pltpu.VMEM((ROWS, FF), BF16),
        pltpu.VMEM((WP, FF), BF16),
        pltpu.VMEM((2, ND, WP, FF), BF16),
        pltpu.VMEM((HALF, FF), BF16),
        pltpu.VMEM((HALF, FF), BF16),
        pltpu.VMEM((NX - 1, 2, WB, FF), BF16),
        pltpu.VMEM((2, ND, WP, FF), BF16),
        pltpu.VMEM((NZ, WP, FF), BF16),
        pltpu.VMEM((ND, NE, CAP, FF), F32),
        pltpu.VMEM((ND, NE, CAP, FF), F32),
        dma((NZ - 1,)),
        dma((NZ - 1,)),
        dma(((NX - 1) * NZ,)),
        dma(((NX - 1) * NZ,)),
        dma((NZ,)),
        dma((2 * ND,)),
        dma(((NX - 1) * 2,)),
        dma(((NX - 1) * 2,)),
        dma((NE * ND,)),
        dma((NE * ND,)),
        dma((NX - 1,)),
        dma((NX - 1,)),
        dma((NZ - 1,)),
        dma((NZ - 1,)),
        dma(((NX - 1) * 2,)),
        dma(((NX - 1) * 2,)),
        dma((2 * ND,)),
        dma((NZ,)),
        dma((NE * ND,)),
        dma((NE * ND,)),
    ]
    dq, dk, dv, hidden, route, dw = pl.pallas_call(
        kernel,
        name="layer_backward",
        out_shape=(
            jax.ShapeDtypeStruct((QRY, GROUP * HD), BF16),
            jax.ShapeDtypeStruct((KEYS, HD), BF16),
            jax.ShapeDtypeStruct((KEYS, HD), BF16),
            jax.ShapeDtypeStruct((TOK, FF), BF16),
            jax.ShapeDtypeStruct((TOK, 1), BF16),
            jax.ShapeDtypeStruct((WS, FF), BF16),
        ),
        in_specs=[smem] + [vmem] * 10,
        out_specs=[vmem] * 6,
        scratch_shapes=scratch,
        compiler_params=pltpu.CompilerParams(
            collective_id=0, has_side_effects=True, vmem_limit_bytes=60 << 20
        ),
    )(
        block_offsets,
        query[0],
        key_rows[0],
        value_rows[0],
        out_grad[0],
        tok_grad,
        hidden_act,
        router_prob.astype(F32)[:, None],
        expert_ids.reshape(1, TOK),
        expert_ids,
        down_weight[0],
    )
    return (dq[None], dk[None], dv[None], hidden, route[:, 0], dw[None])


def solution(mesh):
    in_specs = (
        P("dp", "ctx", "exp"),
        P("dp", "ctx", "exp"),
        P("dp", "ctx", "exp"),
        P("dp", "ctx", "exp"),
        P(),
        P(("ctx", "exp", "dp"), None),
        P(("ctx", "exp", "dp"), None),
        P(("ctx", "exp", "dp")),
        P(("ctx", "exp", "dp"), None),
        P("exp", ("ctx", "dp"), None),
    )
    out_specs = (
        P("dp", "ctx", "exp"),
        P("dp", "ctx", "exp"),
        P("dp", "ctx", "exp"),
        P(("ctx", "exp", "dp"), None),
        P(("ctx", "exp", "dp")),
        P("exp", ("ctx", "dp"), None),
    )
    return jax.shard_map(
        per_device, mesh=mesh, in_specs=in_specs, out_specs=out_specs, check_vma=False
    )
```

```python
import math

import jax
import jax.numpy as jnp
from jax import lax
from jax.experimental import pallas as pl
from jax.experimental.pallas import tpu as pltpu
from jax.sharding import PartitionSpec as P

HD = 128
GROUP = 10
NEG_FILL = -1e30
MESH = pl.DeviceIdType.MESH
F32 = jnp.float32
BF16 = jnp.bfloat16

NX, NZ, NE, ND = 4, 4, 8, 2
KEYS = 256
QRY = 128
COLS = GROUP * QRY
TOK = 128
CAP = 24
D = 6400
HALF = D // 2
FF = 640
PART = (HALF + FF) // 2
WB = 400
WS = 200
WP = 208
SLOTS = NE * CAP
ROWS = ND * SLOTS

NT = (((1,), (1,)), ((), ()))
TN = (((0,), (0,)), ((), ()))


def dot(a, b, dims=(((1,), (0,)), ((), ()))):
    return lax.dot_general(a, b, dims, preferred_element_type=F32)


def kernel(
    off_ref,
    q_ref,
    k_ref,
    v_ref,
    do_ref,
    tok_ref,
    act_ref,
    prob_ref,
    ids_ref,
    w_ref,
    dq_out,
    dk_out,
    dv_out,
    hid_out,
    route_out,
    dw_out,
    kv,
    qs,
    dos,
    stat_m,
    stat_l,
    stat_d,
    p_buf,
    ds_buf,
    dq_acc,
    dkv,
    dkv_o,
    dkv_n,
    dkv_zs,
    dkv_zr,
    perm,
    tsend,
    trecv,
    gbuf,
    abuf,
    wpad,
    wraw,
    wfull,
    wg,
    wg_oa,
    wg_ob,
    wg_n,
    wg_zs,
    wg_zr,
    hsend,
    hrecv,
    kz_s,
    kz_r,
    kx_s,
    kx_r,
    kf_s,
    kf_r,
    wz_s,
    wz_r,
    wx_s,
    wx_r,
    wf_s,
    wf_r,
    tk_s,
    tk_r,
    do_s,
    do_r,
    dn_s,
    dn_r,
    dz_s,
    dz_r,
    go_s,
    go_r,
    gn_s,
    gn_r,
    gz_s,
    gz_r,
    hb_s,
    hb_r,
):
    ctx = lax.axis_index("ctx")
    exp = lax.axis_index("exp")
    core = lax.axis_index("dp")
    z = ctx // NX
    x = ctx % NX
    inv_root = 1.0 / math.sqrt(HD)
    scale2 = inv_root * math.log2(math.e)

    def xpeer(dx):
        return lax.rem(x + dx, NX)

    def zpeer(dz):
        return lax.rem(z + dz, NZ)

    def remote(src, dst, ss, rs, dev):
        return pltpu.make_async_remote_copy(
            src_ref=src, dst_ref=dst, send_sem=ss, recv_sem=rs, device_id=dev, device_id_type=MESH
        )

    step = (1, NX - 1)
    back = (NX - 1, 1)
    near = tuple((z * NX + xpeer(d), exp, core) for d in step)
    sent = []

    def go(copy):
        copy.start()
        sent.append(copy)

    partners = list(near)
    for dz in range(0, NZ):
        for dh in range(ND):
            if dz or dh:
                partners.append((zpeer(dz) * NX + x, exp, lax.rem(core + dh, ND)))
    for de in range(1, NE):
        for dh in range(ND):
            partners.append((ctx, lax.rem(exp + de, NE), lax.rem(core + dh, ND)))
    barrier = pltpu.get_barrier_semaphore()
    for partner in partners:
        pl.semaphore_signal(barrier, inc=1, device_id=partner, device_id_type=MESH)
    pl.semaphore_wait(barrier, len(partners))

    kv[x, z, 0:KEYS] = k_ref[...]
    kv[x, z, KEYS : 2 * KEYS] = v_ref[...]
    halves = (pl.ds(0, KEYS), pl.ds(KEYS, KEYS))

    def kz_copy(dz):
        return remote(
            kv.at[x, z],
            kv.at[x, z],
            kz_s.at[dz - 1],
            kz_r.at[dz - 1],
            (zpeer(dz) * NX + x, exp, core),
        )

    def kx_copy(way, dz, xx):
        at = kv.at[xx, zpeer(NZ - dz)]
        return remote(at, at, kx_s.at[way * NZ + dz], kx_r.at[way * NZ + dz], near[way])

    def kf_copy(way, dz, xx):
        at = kv.at[xx, zpeer(NZ - dz), halves[way]]
        return remote(at, at, kf_s.at[way * NZ + dz], kf_r.at[way * NZ + dz], near[way])

    for dz in (1, 3, 2):
        go(kz_copy(dz))
    for way in range(2):
        go(kx_copy(way, 0, x))

    wpad[0:WS] = w_ref[...]
    wpad[WS:WP] = jnp.zeros((WP - WS, FF), BF16)
    w_core = z // 2
    w_slot = lax.rem(z, 2)
    w_here = core == w_core

    def wz_copy(dz):
        return remote(
            wpad,
            wraw.at[w_slot, core],
            wz_s.at[dz],
            wz_r.at[w_slot * 2 + core],
            (zpeer(dz) * NX + x, exp, w_core),
        )

    for dz in (1, 3, 2):
        go(wz_copy(dz))

    @pl.when(w_here)
    def _():
        wraw[w_slot, core] = wpad[...]

    @pl.when(jnp.logical_not(w_here))
    def _():
        wz_copy(0).start()

    row_at = lax.broadcasted_iota(jnp.int32, (TOK, TOK), 0)
    col_at = lax.broadcasted_iota(jnp.int32, (TOK, TOK), 1)
    eye = row_at == col_at

    def column(row):
        return jnp.sum(jnp.where(eye, row, 0.0), axis=1, keepdims=True)

    ids_row = ids_ref[...]
    ids_f = ids_row.astype(F32)
    prob_col = column(prob_ref[...].astype(F32))
    same = jnp.where((column(ids_f) == ids_f) & (row_at < col_at), 1.0, 0.0)
    rank = jnp.sum(same, axis=0, keepdims=True).astype(jnp.int32)
    target = ids_row * CAP + rank
    slot_at = lax.broadcasted_iota(jnp.int32, (SLOTS, TOK), 0)
    perm[...] = jnp.where(slot_at == target, 1.0, 0.0).astype(BF16)
    scaled_act = (prob_col * act_ref[...].astype(F32)).astype(BF16)

    def tk_copy(de, dh):
        e_to = lax.rem(exp + de, NE)
        h_to = lax.rem(core + dh, ND)
        i = de * ND + dh
        return remote(
            tsend.at[h_to, e_to],
            trecv.at[core, exp],
            tk_s.at[i],
            tk_r.at[i],
            (ctx, e_to, h_to),
        )

    for half in range(ND):
        base = half * HALF
        first = dot(perm[...], tok_ref[:, base : base + PART])
        second = dot(perm[...], tok_ref[:, base + PART : base + HALF])
        third = dot(perm[...], scaled_act)
        for e in range(NE):
            rows = slice(e * CAP, (e + 1) * CAP)
            tsend[half, e, :, 0 : HALF - PART] = jnp.concatenate(
                [first[rows, 0 : HALF - PART], second[rows]], axis=0
            ).astype(BF16)
            tsend[half, e, :, HALF - PART : PART] = jnp.concatenate(
                [first[rows, HALF - PART : PART], third[rows]], axis=0
            ).astype(BF16)
    trecv[core, exp] = tsend[core, exp]
    go(tk_copy(0, 1))
    for de in (4, 2, 6):
        for dh in range(ND):
            go(tk_copy(de, dh))

    for dz in (1, 3, 2):
        kz_copy(dz).wait_recv()
        for way in range(2):
            go(kx_copy(way, dz, x))

    w_halves = ((0, WP), (WP, WB - WP))

    def w_rows(xx, s, part=None):
        start = (s * NX + xx) * WB
        if part is None:
            return pl.ds(pl.multiple_of(start, 16), WB)
        return pl.ds(pl.multiple_of(start + w_halves[part][0], 16), w_halves[part][1])

    def wx_copy(way, s, xx):
        at = wfull.at[w_rows(xx, s)]
        return remote(at, at, wx_s.at[way * 2 + s], wx_r.at[way * 2 + s], near[way])

    def wf_copy(way, s, xx):
        at = wfull.at[w_rows(xx, s, way)]
        return remote(at, at, wf_s.at[way * 2 + s], wf_r.at[way * 2 + s], near[way])

    for s in range(2):
        for h in range(ND):

            @pl.when(jnp.logical_not((2 * core + s == z) & (core == h)))
            def _():
                remote(
                    wpad, wraw.at[s, h], wz_s.at[0], wz_r.at[s * 2 + h], (ctx, exp, core)
                ).wait_recv()

        merged = jnp.concatenate(
            [wraw[s, 0, 0:WS].astype(F32), wraw[s, 1, 0:WS].astype(F32)], axis=0
        )
        wfull[w_rows(x, s)] = merged.astype(BF16)
        for way in range(2):
            go(wx_copy(way, s, x))

    for de in (1, 7, 3, 5):
        for dh in range(ND):
            go(tk_copy(de, dh))

    for h in range(GROUP):
        qs[h * QRY : (h + 1) * QRY] = q_ref[:, h * HD : (h + 1) * HD]
        dos[h * QRY : (h + 1) * QRY] = do_ref[:, h * HD : (h + 1) * HD]

    for dz in (0, 1, 3, 2):
        for way in range(2):
            xx = xpeer(back[way])
            kx_copy(way, dz, xx).wait_recv()
            go(kf_copy(way, dz, xx))

    own_pos = off_ref[ctx] * KEYS + (KEYS - QRY)
    q_pos = own_pos + lax.broadcasted_iota(jnp.int32, (KEYS, QRY), 1)
    k_at = lax.broadcasted_iota(jnp.int32, (KEYS, QRY), 0)
    wide = 2 * QRY

    def bias_of(xx, zz):
        seen = off_ref[zz * NX + xx] * KEYS + k_at <= q_pos
        one = jnp.where(seen, 0.0, NEG_FILL)
        return jnp.concatenate([one, one], axis=1)

    stat_m[...] = jnp.full((1, COLS), NEG_FILL, F32)
    stat_l[...] = jnp.zeros((1, COLS), F32)
    stat_d[...] = jnp.zeros((1, COLS), F32)

    def first_pass(xx, zz):
        bias = bias_of(xx, zz)
        keys = kv[xx, zz, 0:KEYS]
        values = kv[xx, zz, KEYS : 2 * KEYS]
        for g in range(COLS // wide):
            at = slice(g * wide, (g + 1) * wide)
            scores = dot(keys, qs[at], NT) * scale2 + bias
            grads = dot(values, dos[at], NT)
            old = stat_m[:, at]
            peak = jnp.maximum(old, jnp.max(scores, axis=0, keepdims=True))
            shrink = jnp.exp2(old - peak)
            probs = jnp.exp2(scores - peak)
            stat_m[:, at] = peak
            stat_l[:, at] = stat_l[:, at] * shrink + jnp.sum(probs, axis=0, keepdims=True)
            stat_d[:, at] = stat_d[:, at] * shrink + jnp.sum(probs * grads, axis=0, keepdims=True)

    def forward_weights(s):
        for way in range(2):
            xx = xpeer(back[way])
            wx_copy(way, s, xx).wait_recv()
            go(wf_copy(way, s, xx))

    for dx in (0, 1, 3, 2):
        xx = xpeer(dx)
        if dx == 2:
            for dz in range(NZ):
                for way in range(2):
                    kf_copy(way, dz, xx).wait_recv()

        @pl.loop(0, NZ)
        def _(zz):
            first_pass(xx, zz)

    total = stat_l[...]
    stat_m[...] = stat_m[...] + jnp.log2(total)
    stat_d[...] = stat_d[...] / total
    dq_acc[...] = jnp.zeros((HD, COLS), F32)

    def second_pass(xx, zz):
        bias = bias_of(xx, zz)
        keys = kv[xx, zz, 0:KEYS]
        values = kv[xx, zz, KEYS : 2 * KEYS]
        for g in range(COLS // wide):
            at = slice(g * wide, (g + 1) * wide)
            scores = dot(keys, qs[at], NT) * scale2 + bias
            grads = dot(values, dos[at], NT)
            probs = jnp.exp2(scores - stat_m[:, at])
            p_buf[:, at] = probs.astype(BF16)
            ds_buf[:, at] = (probs * (grads - stat_d[:, at])).astype(BF16)
        dkv[xx, 0, zz] = (dot(ds_buf[...], qs[...]) * inv_root).astype(BF16)
        dkv[xx, 1, zz] = dot(p_buf[...], dos[...]).astype(BF16)
        dq_acc[...] += dot(keys, ds_buf[...], TN)

    def do_copy(way):
        return remote(
            dkv.at[xpeer(2), way], dkv_o.at[way], do_s.at[way], do_r.at[way], near[way]
        )

    def dn_copy(way, part):
        i = way * 2 + part
        return remote(
            dkv.at[xpeer(step[way]), part],
            dkv_n.at[way, part],
            dn_s.at[i],
            dn_r.at[i],
            near[way],
        )

    for dx in (2, 1, 3, 0):
        xx = xpeer(dx)

        @pl.loop(0, NZ)
        def _(zz):
            second_pass(xx, zz)

        if dx == 2:
            for way in range(2):
                go(do_copy(way))
            forward_weights(0)
        elif dx:
            way = step.index(dx)
            go(dn_copy(way, 1 - way))
    forward_weights(1)
    for way in range(2):
        do_copy(way).wait_recv()
        xx = xpeer(step[way])
        dkv[xx, way] = (dkv[xx, way].astype(F32) + dkv_o[way].astype(F32)).astype(BF16)
        go(dn_copy(way, way))

    for de in range(NE):
        for dh in range(ND):
            if de or dh:
                tk_copy(de, dh).wait_recv()

    @pl.loop(0, NE)
    def _(i):
        h = i // (NE // 2)
        e = lax.rem(i, NE // 2) * 2
        one = trecv[h, e].astype(F32)
        two = trecv[h, e + 1].astype(F32)
        at = pl.ds(pl.multiple_of(i * 2 * CAP, 2 * CAP), 2 * CAP)
        gbuf[at, 0:PART] = jnp.concatenate([one[0:CAP], two[0:CAP]], axis=0).astype(BF16)
        rest = jnp.concatenate([one[CAP:], two[CAP:]], axis=0).astype(BF16)
        gbuf[at, PART:HALF] = rest[:, 0 : HALF - PART]
        abuf[at] = rest[:, HALF - PART :]

    def go_copy(way, s):
        return remote(
            wg.at[w_rows(xpeer(2), s, way)],
            (wg_oa, wg_ob)[way].at[s],
            go_s.at[way * 2 + s],
            go_r.at[way * 2 + s],
            near[way],
        )

    def gn_copy(way, s, part):
        i = (way * 2 + s) * 2 + part
        return remote(
            wg.at[w_rows(xpeer(step[way]), s, part)],
            wg_n.at[way, s, pl.ds(w_halves[part][0], w_halves[part][1])],
            gn_s.at[i],
            gn_r.at[i],
            near[way],
        )

    def send_grads(s):
        for way in range(2):
            go(go_copy(way, s))
        for way in range(2):
            go(gn_copy(way, s, 1 - way))

    def join_grads(s):
        for way in range(2):
            go_copy(way, s).wait_recv()
            at = w_rows(xpeer(step[way]), s, way)
            theirs = (wg_oa, wg_ob)[way][s]
            wg[at] = (wg[at].astype(F32) + theirs.astype(F32)).astype(BF16)
            go(gn_copy(way, s, way))

    for i in range(HALF // FF):
        at = slice(i * FF, (i + 1) * FF)
        wg[at] = dot(gbuf[:, at], abuf[...], TN).astype(BF16)
        if i == 2:
            send_grads(0)
    send_grads(1)
    join_grads(0)

    for s in range(2):
        for way in range(2):
            wf_copy(way, s, xpeer(2)).wait_recv()
    hidden = dot(gbuf[...], wfull[...])
    for h in range(ND):
        for e in range(NE):
            i = h * NE + e
            hsend[h, e] = hidden[i * CAP : (i + 1) * CAP]

    def hb_copy(de, dh):
        e_to = lax.rem(exp + de, NE)
        h_to = lax.rem(core + dh, ND)
        i = de * ND + dh
        return remote(
            hsend.at[h_to, e_to], hrecv.at[core, exp], hb_s.at[i], hb_r.at[i], (ctx, e_to, h_to)
        )

    for de in range(NE):
        for dh in range(ND):
            if de == 0 and dh == 0:
                hrecv[core, exp] = hsend[core, exp]
            else:
                go(hb_copy(de, dh))
    join_grads(1)

    def dz_copy(dz):
        return remote(
            dkv_zs.at[zpeer(dz)],
            dkv_zr.at[dz - 1],
            dz_s.at[dz - 1],
            dz_r.at[dz - 1],
            (zpeer(dz) * NX + x, exp, core),
        )

    for way in range(2):
        for part in range(2):
            dn_copy(way, part).wait_recv()

    @pl.loop(0, NZ)
    def _(zz):
        for part in range(2):
            sums = dkv[x, part, zz].astype(F32)
            for way in range(2):
                sums = sums + dkv_n[way, part, zz].astype(F32)
            dkv_zs[zz, part] = sums.astype(BF16)

    for dz in (2, 1, 3):
        go(dz_copy(dz))
    for h in range(GROUP):
        dq_out[:, h * HD : (h + 1) * HD] = (
            jnp.transpose(dq_acc[:, h * QRY : (h + 1) * QRY]) * inv_root
        ).astype(BF16)

    def gz_copy(s, h):
        return remote(
            wg_zs.at[s, h],
            wg_zr.at[z],
            gz_s.at[s * 2 + h],
            gz_r.at[z],
            ((2 * core + s) * NX + x, exp, h),
        )

    def sum_grads(s):
        for way in range(2):
            for part in range(2):
                gn_copy(way, s, part).wait_recv()
        sums = wg[w_rows(x, s)].astype(F32)
        for way in range(2):
            sums = sums + wg_n[way, s].astype(F32)
        for h in range(ND):
            wg_zs[s, h, 0:WS] = sums[h * WS : (h + 1) * WS].astype(BF16)
            own = (2 * core + s == z) & (core == h)

            @pl.when(own)
            def _():
                wg_zr[z] = wg_zs[s, h]

            @pl.when(jnp.logical_not(own))
            def _():
                gz_copy(s, h).start()

    wg_zs[:, :, WS:WP] = jnp.zeros((2, ND, WP - WS, FF), BF16)
    sum_grads(0)

    for de in range(NE):
        for dh in range(ND):
            if de or dh:
                hb_copy(de, dh).wait_recv()
    back_rows = jnp.concatenate([hrecv[0, e] + hrecv[1, e] for e in range(NE)], axis=0)
    high = back_rows.astype(BF16)
    low = (back_rows - high.astype(F32)).astype(BF16)
    mine = dot(perm[...], high, TN) + dot(perm[...], low, TN)
    hid_out[...] = (prob_col * mine).astype(BF16)
    route = jnp.sum(act_ref[...].astype(F32) * mine, axis=1, keepdims=True)
    route_out[...] = jnp.sum(jnp.where(eye, route, 0.0), axis=0, keepdims=True).astype(BF16)

    for dz in range(1, NZ):
        dz_copy(dz).wait_recv()
    for part, out in enumerate((dk_out, dv_out)):
        sums = dkv_zs[z, part].astype(F32)
        for i in range(NZ - 1):
            sums = sums + dkv_zr[i, part].astype(F32)
        out[...] = sums.astype(BF16)

    sum_grads(1)
    for zz in range(NZ):

        @pl.when(jnp.logical_not((zz == z) & (core == w_core)))
        def _():
            remote(
                wg_zs.at[0, 0], wg_zr.at[zz], gz_s.at[0], gz_r.at[zz], (ctx, exp, core)
            ).wait_recv()

    sums = wg_zr[0].astype(F32)
    for zz in range(1, NZ):
        sums = sums + wg_zr[zz].astype(F32)
    dw_out[...] = sums[0:WS].astype(BF16)

    for copy in sent:
        copy.wait_send()

    @pl.when(jnp.logical_not(w_here))
    def _():
        wz_copy(0).wait_send()

    for s in range(2):
        for h in range(ND):

            @pl.when(jnp.logical_not((2 * core + s == z) & (core == h)))
            def _():
                gz_copy(s, h).wait_send()


def finish(*refs):
    count = len(refs) // 2
    for source, out in zip(refs[:count], refs[count:]):
        out[...] = source[...]


def per_device(
    query,
    key_rows,
    value_rows,
    out_grad,
    block_offsets,
    tok_grad,
    hidden_act,
    router_prob,
    expert_ids,
    down_weight,
):
    vmem = pl.BlockSpec(memory_space=pltpu.VMEM)
    smem = pl.BlockSpec(memory_space=pltpu.SMEM)
    dma = pltpu.SemaphoreType.DMA
    scratch = [
        pltpu.VMEM((NX, NZ, 2 * KEYS, HD), BF16),
        pltpu.VMEM((COLS, HD), BF16),
        pltpu.VMEM((COLS, HD), BF16),
        pltpu.VMEM((1, COLS), F32),
        pltpu.VMEM((1, COLS), F32),
        pltpu.VMEM((1, COLS), F32),
        pltpu.VMEM((KEYS, COLS), BF16),
        pltpu.VMEM((KEYS, COLS), BF16),
        pltpu.VMEM((HD, COLS), F32),
        pltpu.VMEM((NX, 2, NZ, KEYS, HD), BF16),
        pltpu.VMEM((2, NZ, KEYS, HD), BF16),
        pltpu.VMEM((2, 2, NZ, KEYS, HD), BF16),
        pltpu.VMEM((NZ, 2, KEYS, HD), BF16),
        pltpu.VMEM((NZ - 1, 2, KEYS, HD), BF16),
        pltpu.VMEM((SLOTS, TOK), BF16),
        pltpu.VMEM((ND, NE, 2 * CAP, PART), BF16),
        pltpu.VMEM((ND, NE, 2 * CAP, PART), BF16),
        pltpu.VMEM((ROWS, HALF), BF16),
        pltpu.VMEM((ROWS, FF), BF16),
        pltpu.VMEM((WP, FF), BF16),
        pltpu.VMEM((2, ND, WP, FF), BF16),
        pltpu.VMEM((HALF, FF), BF16),
        pltpu.VMEM((HALF, FF), BF16),
        pltpu.VMEM((2, WP, FF), BF16),
        pltpu.VMEM((2, WB - WP, FF), BF16),
        pltpu.VMEM((2, 2, WB, FF), BF16),
        pltpu.VMEM((2, ND, WP, FF), BF16),
        pltpu.VMEM((NZ, WP, FF), BF16),
        pltpu.VMEM((ND, NE, CAP, FF), F32),
        pltpu.VMEM((ND, NE, CAP, FF), F32),
    ]
    for size in (
        NZ - 1,
        2 * NZ,
        2 * NZ,
        NZ,
        4,
        4,
        NE * ND,
        2,
        4,
        NZ - 1,
        4,
        8,
        NZ,
        NE * ND,
    ):
        scratch += [dma((size,)), dma((size,))]
    shapes = (
        jax.ShapeDtypeStruct((QRY, GROUP * HD), BF16),
        jax.ShapeDtypeStruct((KEYS, HD), BF16),
        jax.ShapeDtypeStruct((KEYS, HD), BF16),
        jax.ShapeDtypeStruct((TOK, FF), BF16),
        jax.ShapeDtypeStruct((1, TOK), BF16),
        jax.ShapeDtypeStruct((WS, FF), BF16),
    )
    results = pl.pallas_call(
        kernel,
        name="layer_backward",
        out_shape=shapes,
        in_specs=[smem] + [vmem] * 9,
        out_specs=[vmem] * 6,
        scratch_shapes=scratch,
        compiler_params=pltpu.CompilerParams(
            collective_id=0, has_side_effects=True, vmem_limit_bytes=60 << 20
        ),
    )(
        block_offsets,
        query[0],
        key_rows[0],
        value_rows[0],
        out_grad[0],
        tok_grad,
        hidden_act,
        router_prob.reshape(1, TOK),
        expert_ids.reshape(1, TOK),
        down_weight[0],
    )
    dq, dk, dv, hidden, route, dw = pl.pallas_call(
        finish, name="finish", out_shape=shapes, in_specs=[vmem] * 6, out_specs=[vmem] * 6
    )(*results)
    return (dq[None], dk[None], dv[None], hidden, route[0], dw[None])


def solution(mesh):
    in_specs = (
        P("dp", "ctx", "exp"),
        P("dp", "ctx", "exp"),
        P("dp", "ctx", "exp"),
        P("dp", "ctx", "exp"),
        P(),
        P(("ctx", "exp", "dp"), None),
        P(("ctx", "exp", "dp"), None),
        P(("ctx", "exp", "dp")),
        P(("ctx", "exp", "dp"), None),
        P("exp", ("ctx", "dp"), None),
    )
    out_specs = (
        P("dp", "ctx", "exp"),
        P("dp", "ctx", "exp"),
        P("dp", "ctx", "exp"),
        P(("ctx", "exp", "dp"), None),
        P(("ctx", "exp", "dp")),
        P("exp", ("ctx", "dp"), None),
    )
    return jax.shard_map(
        per_device, mesh=mesh, in_specs=in_specs, out_specs=out_specs, check_vma=False
    )
```

```python
import math

import jax
import jax.numpy as jnp
from jax import lax
from jax.experimental import pallas as pl
from jax.experimental.pallas import tpu as pltpu
from jax.sharding import PartitionSpec as P

HD = 128
GROUP = 10
NEG_FILL = -1e30
MESH = pl.DeviceIdType.MESH
F32 = jnp.float32
BF16 = jnp.bfloat16

NX, NZ, NE, ND = 4, 4, 8, 2
KEYS = 256
QRY = 128
COLS = GROUP * QRY
TOK = 128
CAP = 24
D = 6400
HALF = D // 2
FF = 640
PART = (HALF + FF) // 2
WB = 400
WS = 200
WP = 208
SLOTS = NE * CAP
ROWS = ND * SLOTS

NT = (((1,), (1,)), ((), ()))
TN = (((0,), (0,)), ((), ()))


def dot(a, b, dims=(((1,), (0,)), ((), ()))):
    return lax.dot_general(a, b, dims, preferred_element_type=F32)


def kernel(
    off_ref,
    q_ref,
    k_ref,
    v_ref,
    do_ref,
    tok_ref,
    act_ref,
    prob_ref,
    ids_ref,
    w_ref,
    dq_out,
    dk_out,
    dv_out,
    hid_out,
    route_out,
    dw_out,
    kv,
    qs,
    dos,
    stat_m,
    stat_l,
    stat_d,
    p_buf,
    ds_buf,
    dq_acc,
    dkv,
    dkv_o,
    dkv_n,
    dkv_zs,
    dkv_zr,
    perm,
    tsend,
    trecv,
    gbuf,
    abuf,
    wpad,
    wraw,
    wfull,
    wg,
    wg_oa,
    wg_ob,
    wg_n,
    wg_zs,
    wg_zr,
    hsend,
    hother,
    hsum,
    hrecv,
    kz_s,
    kz_r,
    kg_s,
    kg_r,
    kx_s,
    kx_r,
    kf_s,
    kf_r,
    wz_s,
    wz_r,
    wg_s,
    wg_r,
    wx_s,
    wx_r,
    wf_s,
    wf_r,
    tk_s,
    tk_r,
    do_s,
    do_r,
    dn_s,
    dn_r,
    dz_s,
    dz_r,
    go_s,
    go_r,
    gn_s,
    gn_r,
    gz_s,
    gz_r,
    hx_s,
    hx_r,
    hb_s,
    hb_r,
):
    ctx = lax.axis_index("ctx")
    exp = lax.axis_index("exp")
    core = lax.axis_index("dp")
    z = ctx // NX
    x = ctx % NX
    inv_root = 1.0 / math.sqrt(HD)
    scale2 = inv_root * math.log2(math.e)

    def xpeer(dx):
        return lax.rem(x + dx, NX)

    def zpeer(dz):
        return lax.rem(z + dz, NZ)

    def remote(src, dst, ss, rs, dev):
        return pltpu.make_async_remote_copy(
            src_ref=src, dst_ref=dst, send_sem=ss, recv_sem=rs, device_id=dev, device_id_type=MESH
        )

    step = (1, NX - 1)
    back = (NX - 1, 1)
    near = tuple((z * NX + xpeer(d), exp, core) for d in step)
    sent = []

    def go(copy):
        copy.start()
        sent.append(copy)

    partners = list(near)
    for dz in range(0, NZ):
        for dh in range(ND):
            if dz or dh:
                partners.append((zpeer(dz) * NX + x, exp, lax.rem(core + dh, ND)))
    for de in range(1, NE):
        for dh in range(ND):
            partners.append((ctx, lax.rem(exp + de, NE), lax.rem(core + dh, ND)))
    barrier = pltpu.get_barrier_semaphore()
    for partner in partners:
        pl.semaphore_signal(barrier, inc=1, device_id=partner, device_id_type=MESH)
    pl.semaphore_wait(barrier, len(partners))

    kv[x, z, 0:KEYS] = k_ref[...]
    kv[x, z, KEYS : 2 * KEYS] = v_ref[...]
    halves = (pl.ds(0, KEYS), pl.ds(KEYS, KEYS))

    above = tuple((zpeer(d) * NX + x, exp, core) for d in step)

    def kz_copy(way, zz):
        at = kv.at[x, zz]
        return remote(at, at, kz_s.at[way], kz_r.at[way], above[way])

    def kg_copy(way, zz):
        at = kv.at[x, zz, halves[way]]
        return remote(at, at, kg_s.at[way], kg_r.at[way], above[way])

    def kx_copy(way, dz, xx):
        at = kv.at[xx, zpeer(NZ - dz)]
        return remote(at, at, kx_s.at[way * NZ + dz], kx_r.at[way * NZ + dz], near[way])

    def kf_copy(way, dz, xx):
        at = kv.at[xx, zpeer(NZ - dz), halves[way]]
        return remote(at, at, kf_s.at[way * NZ + dz], kf_r.at[way * NZ + dz], near[way])

    for way in range(2):
        go(kz_copy(way, z))
    for way in range(2):
        go(kx_copy(way, 0, x))

    wpad[0:WS] = w_ref[...]
    wpad[WS:WP] = jnp.zeros((WP - WS, FF), BF16)
    w_core = z // 2
    w_slot = lax.rem(z, 2)
    w_here = core == w_core

    def wz_copy(dz):
        return remote(
            wpad,
            wraw.at[w_slot, core],
            wz_s.at[dz],
            wz_r.at[w_slot * 2 + core],
            (zpeer(dz) * NX + x, exp, w_core),
        )

    for dz in step:
        go(wz_copy(dz))

    @pl.when(w_here)
    def _():
        wraw[w_slot, core] = wpad[...]

    @pl.when(jnp.logical_not(w_here))
    def _():
        wz_copy(0).start()

    z_halves = (pl.ds(0, 112), pl.ds(112, WP - 112))

    def wz_wait(s, h):
        remote(wpad, wraw.at[s, h], wz_s.at[0], wz_r.at[s * 2 + h], (ctx, exp, core)).wait_recv()

    def wf_zcopy(way, zz, h):
        at = wraw.at[lax.rem(zz, 2), h, z_halves[way]]
        i = way * 2 + h
        return remote(at, at, wg_s.at[i], wg_r.at[i], above[way])

    w_halves = ((0, WP), (WP, WB - WP))

    def w_rows(xx, s, part=None):
        start = (s * NX + xx) * WB
        if part is None:
            return pl.ds(pl.multiple_of(start, 16), WB)
        return pl.ds(pl.multiple_of(start + w_halves[part][0], 16), w_halves[part][1])

    def wx_copy(way, s, xx):
        at = wfull.at[w_rows(xx, s)]
        return remote(at, at, wx_s.at[way * 2 + s], wx_r.at[way * 2 + s], near[way])

    def wf_copy(way, s, xx):
        at = wfull.at[w_rows(xx, s, way)]
        return remote(at, at, wf_s.at[way * 2 + s], wf_r.at[way * 2 + s], near[way])

    def place_weights(s):
        merged = jnp.concatenate(
            [wraw[s, 0, 0:WS].astype(F32), wraw[s, 1, 0:WS].astype(F32)], axis=0
        )
        wfull[w_rows(x, s)] = merged.astype(BF16)
        for way in range(2):
            wx_copy(way, s, x).start()

    w_other = lax.rem(z + 1, 2)
    w_first = lax.rem(z + (core - w_core) * (core - w_core), 2)

    row_at = lax.broadcasted_iota(jnp.int32, (TOK, TOK), 0)
    col_at = lax.broadcasted_iota(jnp.int32, (TOK, TOK), 1)
    eye = row_at == col_at

    def column(row):
        return jnp.sum(jnp.where(eye, row, 0.0), axis=1, keepdims=True)

    ids_row = ids_ref[...]
    ids_f = ids_row.astype(F32)
    prob_col = column(prob_ref[...].astype(F32))
    same = jnp.where((column(ids_f) == ids_f) & (row_at < col_at), 1.0, 0.0)
    rank = jnp.sum(same, axis=0, keepdims=True).astype(jnp.int32)
    target = ids_row * CAP + rank
    slot_at = lax.broadcasted_iota(jnp.int32, (SLOTS, TOK), 0)
    perm[...] = jnp.where(slot_at == target, 1.0, 0.0).astype(BF16)
    scaled_act = (prob_col * act_ref[...].astype(F32)).astype(BF16)

    def tk_copy(de, dh):
        e_to = lax.rem(exp + de, NE)
        h_to = lax.rem(core + dh, ND)
        i = de * ND + dh
        return remote(
            tsend.at[h_to, e_to],
            trecv.at[core, exp],
            tk_s.at[i],
            tk_r.at[i],
            (ctx, e_to, h_to),
        )

    for half in range(ND):
        base = half * HALF
        first = dot(perm[...], tok_ref[:, base : base + PART])
        second = dot(perm[...], tok_ref[:, base + PART : base + HALF])
        third = dot(perm[...], scaled_act)
        for e in range(NE):
            rows = slice(e * CAP, (e + 1) * CAP)
            tsend[half, e, :, 0 : HALF - PART] = jnp.concatenate(
                [first[rows, 0 : HALF - PART], second[rows]], axis=0
            ).astype(BF16)
            tsend[half, e, :, HALF - PART : PART] = jnp.concatenate(
                [first[rows, HALF - PART : PART], third[rows]], axis=0
            ).astype(BF16)

    @pl.when(w_here)
    def _():
        wz_wait(w_slot, 1 - core)
        place_weights(w_slot)

    trecv[core, exp] = tsend[core, exp]
    go(tk_copy(0, 1))
    for de in (4, 2, 6):
        for dh in range(ND):
            go(tk_copy(de, dh))

    for way in range(2):
        zz = zpeer(back[way])
        kz_copy(way, zz).wait_recv()
        go(kg_copy(way, zz))
        for to in range(2):
            go(kx_copy(to, back[1 - way], x))
    for way in range(2):
        zz = zpeer(back[way])

        @pl.when(core == zz // 2)
        def _():
            for h in range(ND):
                wz_wait(lax.rem(zz, 2), h)
                wf_zcopy(way, zz, h).start()

    for way in range(2):
        kg_copy(way, zpeer(2)).wait_recv()
    for way in range(2):
        go(kx_copy(way, 2, x))
    place_weights(w_other)

    for h in range(GROUP):
        qs[h * QRY : (h + 1) * QRY] = q_ref[:, h * HD : (h + 1) * HD]
        dos[h * QRY : (h + 1) * QRY] = do_ref[:, h * HD : (h + 1) * HD]

    for dz in (0, 1, 3, 2):
        for way in range(2):
            xx = xpeer(back[way])
            kx_copy(way, dz, xx).wait_recv()
            go(kf_copy(way, dz, xx))

    own_pos = off_ref[ctx] * KEYS + (KEYS - QRY)
    q_pos = own_pos + lax.broadcasted_iota(jnp.int32, (KEYS, QRY), 1)
    k_at = lax.broadcasted_iota(jnp.int32, (KEYS, QRY), 0)
    wide = 2 * QRY

    def bias_of(xx, zz):
        seen = off_ref[zz * NX + xx] * KEYS + k_at <= q_pos
        one = jnp.where(seen, 0.0, NEG_FILL)
        return jnp.concatenate([one, one], axis=1)

    stat_m[...] = jnp.full((1, COLS), NEG_FILL, F32)
    stat_l[...] = jnp.zeros((1, COLS), F32)
    stat_d[...] = jnp.zeros((1, COLS), F32)

    def first_pass(xx, zz):
        bias = bias_of(xx, zz)
        keys = kv[xx, zz, 0:KEYS]
        values = kv[xx, zz, KEYS : 2 * KEYS]
        for g in range(COLS // wide):
            at = slice(g * wide, (g + 1) * wide)
            scores = dot(keys, qs[at], NT) * scale2 + bias
            grads = dot(values, dos[at], NT)
            old = stat_m[:, at]
            peak = jnp.maximum(old, jnp.max(scores, axis=0, keepdims=True))
            shrink = jnp.exp2(old - peak)
            probs = jnp.exp2(scores - peak)
            stat_m[:, at] = peak
            stat_l[:, at] = stat_l[:, at] * shrink + jnp.sum(probs, axis=0, keepdims=True)
            stat_d[:, at] = stat_d[:, at] * shrink + jnp.sum(probs * grads, axis=0, keepdims=True)

    def forward_weights(s):
        for way in range(2):
            xx = xpeer(back[way])
            wx_copy(way, s, xx).wait_recv()
            go(wf_copy(way, s, xx))

    for dx in (0, 1, 3, 2):
        xx = xpeer(dx)
        if dx == 1:
            @pl.when(jnp.logical_not(w_here))
            def _():
                for h in range(ND):
                    for way in range(2):
                        wf_zcopy(way, zpeer(2), h).wait_recv()
                place_weights(w_slot)

            for de in (1, 7, 3, 5):
                for dh in range(ND):
                    go(tk_copy(de, dh))
        if dx == 2:
            for dz in range(NZ):
                for way in range(2):
                    kf_copy(way, dz, xx).wait_recv()

        @pl.loop(0, NZ)
        def _(zz):
            first_pass(xx, zz)

    total = stat_l[...]
    stat_m[...] = stat_m[...] + jnp.log2(total)
    stat_d[...] = stat_d[...] / total
    dq_acc[...] = jnp.zeros((HD, COLS), F32)

    def second_pass(xx, zz):
        bias = bias_of(xx, zz)
        keys = kv[xx, zz, 0:KEYS]
        values = kv[xx, zz, KEYS : 2 * KEYS]
        for g in range(COLS // wide):
            at = slice(g * wide, (g + 1) * wide)
            scores = dot(keys, qs[at], NT) * scale2 + bias
            grads = dot(values, dos[at], NT)
            probs = jnp.exp2(scores - stat_m[:, at])
            p_buf[:, at] = probs.astype(BF16)
            ds_buf[:, at] = (probs * (grads - stat_d[:, at])).astype(BF16)
        dkv[xx, 0, zz] = (dot(ds_buf[...], qs[...]) * inv_root).astype(BF16)
        dkv[xx, 1, zz] = dot(p_buf[...], dos[...]).astype(BF16)
        dq_acc[...] += dot(keys, ds_buf[...], TN)

    def do_copy(way):
        return remote(
            dkv.at[xpeer(2), way], dkv_o.at[way], do_s.at[way], do_r.at[way], near[way]
        )

    def dn_copy(way, part):
        i = way * 2 + part
        return remote(
            dkv.at[xpeer(step[way]), part],
            dkv_n.at[way, part],
            dn_s.at[i],
            dn_r.at[i],
            near[way],
        )

    def pair(h, other, j):
        return (h * 2 + other) * 2 + j, lax.rem(exp + other, 2) + 4 * j

    def unpack(other):
        for de in range(NE):
            for dh in range(ND):
                if (de or dh) and de % 2 == other:
                    tk_copy(de, dh).wait_recv()

        @pl.loop(0, 2 * ND)
        def _(i):
            h = i // 2
            slot, e = pair(h, other, lax.rem(i, 2))
            one = trecv[h, e].astype(F32)
            two = trecv[h, e + 2].astype(F32)
            at = pl.ds(pl.multiple_of(slot * 2 * CAP, 2 * CAP), 2 * CAP)
            gbuf[at, 0:PART] = jnp.concatenate([one[0:CAP], two[0:CAP]], axis=0).astype(BF16)
            rest = jnp.concatenate([one[CAP:], two[CAP:]], axis=0).astype(BF16)
            gbuf[at, PART:HALF] = rest[:, 0 : HALF - PART]
            abuf[at] = rest[:, HALF - PART :]

    def go_copy(way, s):
        return remote(
            wg.at[w_rows(xpeer(2), s, way)],
            (wg_oa, wg_ob)[way].at[s],
            go_s.at[way * 2 + s],
            go_r.at[way * 2 + s],
            near[way],
        )

    def gn_copy(way, s, part):
        i = (way * 2 + s) * 2 + part
        return remote(
            wg.at[w_rows(xpeer(step[way]), s, part)],
            wg_n.at[way, s, pl.ds(w_halves[part][0], w_halves[part][1])],
            gn_s.at[i],
            gn_r.at[i],
            near[way],
        )

    def send_grads(s):
        for way in range(2):
            go(go_copy(way, s))
        for way in range(2):
            go(gn_copy(way, s, 1 - way))

    def join_grads(s):
        for way in range(2):
            go_copy(way, s).wait_recv()
            at = w_rows(xpeer(step[way]), s, way)
            theirs = (wg_oa, wg_ob)[way][s]
            wg[at] = (wg[at].astype(F32) + theirs.astype(F32)).astype(BF16)
            go(gn_copy(way, s, way))

    def weight_grads(chunks):
        for i in chunks:
            at = slice(i * FF, (i + 1) * FF)
            wg[at] = dot(gbuf[:, at], abuf[...], TN).astype(BF16)

    for dx in (2, 1, 3, 0):
        xx = xpeer(dx)
        if dx == 0:
            for way in range(2):
                do_copy(way).wait_recv()
                to = xpeer(step[way])
                dkv[to, way] = (dkv[to, way].astype(F32) + dkv_o[way].astype(F32)).astype(BF16)
                go(dn_copy(way, way))
            unpack(1)
            weight_grads(range(3))
            send_grads(0)
            weight_grads(range(3, HALF // FF))

        @pl.loop(0, NZ)
        def _(zz):
            second_pass(xx, zz)

        if dx == 2:
            for way in range(2):
                go(do_copy(way))
            forward_weights(w_first)
        elif dx:
            way = step.index(dx)
            go(dn_copy(way, 1 - way))
            if dx == 1:
                forward_weights(1 - w_first)
                unpack(0)
    join_grads(0)
    send_grads(1)

    def dz_copy(dz):
        return remote(
            dkv_zs.at[zpeer(dz)],
            dkv_zr.at[dz - 1],
            dz_s.at[dz - 1],
            dz_r.at[dz - 1],
            (zpeer(dz) * NX + x, exp, core),
        )

    for way in range(2):
        for part in range(2):
            dn_copy(way, part).wait_recv()

    @pl.loop(0, NZ)
    def _(zz):
        for part in range(2):
            sums = dkv[x, part, zz].astype(F32)
            for way in range(2):
                sums = sums + dkv_n[way, part, zz].astype(F32)
            dkv_zs[zz, part] = sums.astype(BF16)

    for dz in (2, 1, 3):
        go(dz_copy(dz))
    for s in range(2):
        for way in range(2):
            wf_copy(way, s, xpeer(2)).wait_recv()
    hidden = dot(gbuf[...], wfull[...])
    for h in range(ND):
        for other in range(2):
            for j in range(2):
                slot, e = pair(h, other, j)
                for two in range(2):
                    row = (slot * 2 + two) * CAP
                    hsend[h, e + 2 * two] = hidden[row : row + CAP]

    hx_copy = remote(
        hsend.at[1 - core], hother, hx_s.at[0], hx_r.at[0], (ctx, exp, 1 - core)
    )
    go(hx_copy)

    def hb_copy(de):
        e_to = lax.rem(exp + de, NE)
        return remote(hsum.at[e_to], hrecv.at[exp], hb_s.at[de], hb_r.at[de], (ctx, e_to, core))

    hx_copy.wait_recv()
    hsum[...] = hsend[core] + hother[...]
    hrecv[exp] = hsum[exp]
    for de in (1, 7, 3, 5, 4, 2, 6):
        go(hb_copy(de))
    join_grads(1)

    def gz_copy(s, h):
        return remote(
            wg_zs.at[s, h],
            wg_zr.at[z],
            gz_s.at[s * 2 + h],
            gz_r.at[z],
            ((2 * core + s) * NX + x, exp, h),
        )

    def sum_grads(s):
        for way in range(2):
            for part in range(2):
                gn_copy(way, s, part).wait_recv()
        sums = wg[w_rows(x, s)].astype(F32)
        for way in range(2):
            sums = sums + wg_n[way, s].astype(F32)
        for h in range(ND):
            wg_zs[s, h, 0:WS] = sums[h * WS : (h + 1) * WS].astype(BF16)
            own = (2 * core + s == z) & (core == h)

            @pl.when(own)
            def _():
                wg_zr[z] = wg_zs[s, h]

            @pl.when(jnp.logical_not(own))
            def _():
                gz_copy(s, h).start()

    wg_zs[:, :, WS:WP] = jnp.zeros((2, ND, WP - WS, FF), BF16)
    sum_grads(0)

    sum_grads(1)
    for h in range(GROUP):
        dq_out[:, h * HD : (h + 1) * HD] = (
            jnp.transpose(dq_acc[:, h * QRY : (h + 1) * QRY]) * inv_root
        ).astype(BF16)

    for de in range(1, NE):
        hb_copy(de).wait_recv()
    back_rows = jnp.concatenate([hrecv[e] for e in range(NE)], axis=0)
    high = back_rows.astype(BF16)
    low = (back_rows - high.astype(F32)).astype(BF16)
    mine = dot(perm[...], high, TN) + dot(perm[...], low, TN)
    hid_out[...] = (prob_col * mine).astype(BF16)
    route = jnp.sum(act_ref[...].astype(F32) * mine, axis=1, keepdims=True)
    route_out[...] = jnp.sum(jnp.where(eye, route, 0.0), axis=0, keepdims=True).astype(BF16)

    for dz in range(1, NZ):
        dz_copy(dz).wait_recv()
    for part, out in enumerate((dk_out, dv_out)):
        sums = dkv_zs[z, part].astype(F32)
        for i in range(NZ - 1):
            sums = sums + dkv_zr[i, part].astype(F32)
        out[...] = sums.astype(BF16)

    for zz in range(NZ):

        @pl.when(jnp.logical_not((zz == z) & (core == w_core)))
        def _():
            remote(
                wg_zs.at[0, 0], wg_zr.at[zz], gz_s.at[0], gz_r.at[zz], (ctx, exp, core)
            ).wait_recv()

    sums = wg_zr[0].astype(F32)
    for zz in range(1, NZ):
        sums = sums + wg_zr[zz].astype(F32)
    dw_out[...] = sums[0:WS].astype(BF16)

    for copy in sent:
        copy.wait_send()
    for way in range(2):
        for s in range(2):
            wx_copy(way, s, x).wait_send()

    @pl.when(jnp.logical_not(w_here))
    def _():
        wz_copy(0).wait_send()

    for way in range(2):
        zz = zpeer(back[way])

        @pl.when(core == zz // 2)
        def _():
            for h in range(ND):
                wf_zcopy(way, zz, h).wait_send()

    for s in range(2):
        for h in range(ND):

            @pl.when(jnp.logical_not((2 * core + s == z) & (core == h)))
            def _():
                gz_copy(s, h).wait_send()


def finish(*refs):
    count = len(refs) // 2
    for source, out in zip(refs[:count], refs[count:]):
        out[...] = source[...]


def per_device(
    query,
    key_rows,
    value_rows,
    out_grad,
    block_offsets,
    tok_grad,
    hidden_act,
    router_prob,
    expert_ids,
    down_weight,
):
    vmem = pl.BlockSpec(memory_space=pltpu.VMEM)
    smem = pl.BlockSpec(memory_space=pltpu.SMEM)
    dma = pltpu.SemaphoreType.DMA
    scratch = [
        pltpu.VMEM((NX, NZ, 2 * KEYS, HD), BF16),
        pltpu.VMEM((COLS, HD), BF16),
        pltpu.VMEM((COLS, HD), BF16),
        pltpu.VMEM((1, COLS), F32),
        pltpu.VMEM((1, COLS), F32),
        pltpu.VMEM((1, COLS), F32),
        pltpu.VMEM((KEYS, COLS), BF16),
        pltpu.VMEM((KEYS, COLS), BF16),
        pltpu.VMEM((HD, COLS), F32),
        pltpu.VMEM((NX, 2, NZ, KEYS, HD), BF16),
        pltpu.VMEM((2, NZ, KEYS, HD), BF16),
        pltpu.VMEM((2, 2, NZ, KEYS, HD), BF16),
        pltpu.VMEM((NZ, 2, KEYS, HD), BF16),
        pltpu.VMEM((NZ - 1, 2, KEYS, HD), BF16),
        pltpu.VMEM((SLOTS, TOK), BF16),
        pltpu.VMEM((ND, NE, 2 * CAP, PART), BF16),
        pltpu.VMEM((ND, NE, 2 * CAP, PART), BF16),
        pltpu.VMEM((ROWS, HALF), BF16),
        pltpu.VMEM((ROWS, FF), BF16),
        pltpu.VMEM((WP, FF), BF16),
        pltpu.VMEM((2, ND, WP, FF), BF16),
        pltpu.VMEM((HALF, FF), BF16),
        pltpu.VMEM((HALF, FF), BF16),
        pltpu.VMEM((2, WP, FF), BF16),
        pltpu.VMEM((2, WB - WP, FF), BF16),
        pltpu.VMEM((2, 2, WB, FF), BF16),
        pltpu.VMEM((2, ND, WP, FF), BF16),
        pltpu.VMEM((NZ, WP, FF), BF16),
        pltpu.VMEM((ND, NE, CAP, FF), F32),
        pltpu.VMEM((NE, CAP, FF), F32),
        pltpu.VMEM((NE, CAP, FF), F32),
        pltpu.VMEM((NE, CAP, FF), F32),
    ]
    for size in (
        2,
        2,
        2 * NZ,
        2 * NZ,
        NZ,
        4,
        4,
        4,
        NE * ND,
        2,
        4,
        NZ - 1,
        4,
        8,
        NZ,
        1,
        NE,
    ):
        scratch += [dma((size,)), dma((size,))]
    shapes = (
        jax.ShapeDtypeStruct((QRY, GROUP * HD), BF16),
        jax.ShapeDtypeStruct((KEYS, HD), BF16),
        jax.ShapeDtypeStruct((KEYS, HD), BF16),
        jax.ShapeDtypeStruct((TOK, FF), BF16),
        jax.ShapeDtypeStruct((1, TOK), BF16),
        jax.ShapeDtypeStruct((WS, FF), BF16),
    )
    results = pl.pallas_call(
        kernel,
        name="layer_backward",
        out_shape=shapes,
        in_specs=[smem] + [vmem] * 9,
        out_specs=[vmem] * 6,
        scratch_shapes=scratch,
        compiler_params=pltpu.CompilerParams(
            collective_id=0, has_side_effects=True, vmem_limit_bytes=60 << 20
        ),
    )(
        block_offsets,
        query[0],
        key_rows[0],
        value_rows[0],
        out_grad[0],
        tok_grad,
        hidden_act,
        router_prob.reshape(1, TOK),
        expert_ids.reshape(1, TOK),
        down_weight[0],
    )
    dq, dk, dv, hidden, route, dw = pl.pallas_call(
        finish, name="finish", out_shape=shapes, in_specs=[vmem] * 6, out_specs=[vmem] * 6
    )(*results)
    return (dq[None], dk[None], dv[None], hidden, route[0], dw[None])


def solution(mesh):
    in_specs = (
        P("dp", "ctx", "exp"),
        P("dp", "ctx", "exp"),
        P("dp", "ctx", "exp"),
        P("dp", "ctx", "exp"),
        P(),
        P(("ctx", "exp", "dp"), None),
        P(("ctx", "exp", "dp"), None),
        P(("ctx", "exp", "dp")),
        P(("ctx", "exp", "dp"), None),
        P("exp", ("ctx", "dp"), None),
    )
    out_specs = (
        P("dp", "ctx", "exp"),
        P("dp", "ctx", "exp"),
        P("dp", "ctx", "exp"),
        P(("ctx", "exp", "dp"), None),
        P(("ctx", "exp", "dp")),
        P("exp", ("ctx", "dp"), None),
    )
    return jax.shard_map(
        per_device, mesh=mesh, in_specs=in_specs, out_specs=out_specs, check_vma=False
    )
```

```python
import math

import jax
import jax.numpy as jnp
from jax import lax
from jax.experimental import pallas as pl
from jax.experimental.pallas import tpu as pltpu
from jax.sharding import PartitionSpec as P

HD = 128
GROUP = 10
NEG_FILL = -1e30
MESH = pl.DeviceIdType.MESH
F32 = jnp.float32
BF16 = jnp.bfloat16

NX, NZ, NE, ND = 4, 4, 8, 2
KEYS = 256
QRY = 128
COLS = GROUP * QRY
TOK = 128
CAP = 24
D = 6400
HALF = D // 2
FF = 640
PART = (HALF + FF) // 2
WB = 400
WS = 200
WP = 208
SLOTS = NE * CAP
ROWS = ND * SLOTS

NT = (((1,), (1,)), ((), ()))
TN = (((0,), (0,)), ((), ()))


def dot(a, b, dims=(((1,), (0,)), ((), ()))):
    return lax.dot_general(a, b, dims, preferred_element_type=F32)


def kernel(
    off_ref,
    q_ref,
    k_ref,
    v_ref,
    do_ref,
    tok_ref,
    act_ref,
    prob_ref,
    ids_ref,
    w_ref,
    dq_out,
    dk_out,
    dv_out,
    hid_out,
    route_out,
    dw_out,
    kv,
    qs,
    dos,
    stat_m,
    stat_l,
    stat_d,
    p_buf,
    ds_buf,
    dq_acc,
    dkv,
    dkv_o,
    dkv_n,
    dkv_zs,
    dkv_zr,
    perm,
    tsend,
    trecv,
    gbuf,
    abuf,
    wpad,
    wraw,
    wfull,
    wg,
    wg_oa,
    wg_ob,
    wg_n,
    wg_zs,
    wg_zr,
    hsend,
    hother,
    hsum,
    hrecv,
    kz_s,
    kz_r,
    kg_s,
    kg_r,
    kx_s,
    kx_r,
    kf_s,
    kf_r,
    wz_s,
    wz_r,
    wg_s,
    wg_r,
    wx_s,
    wx_r,
    wf_s,
    wf_r,
    tk_s,
    tk_r,
    do_s,
    do_r,
    dn_s,
    dn_r,
    dz_s,
    dz_r,
    go_s,
    go_r,
    gn_s,
    gn_r,
    gz_s,
    gz_r,
    hx_s,
    hx_r,
    hb_s,
    hb_r,
):
    ctx = lax.axis_index("ctx")
    exp = lax.axis_index("exp")
    core = lax.axis_index("dp")
    z = ctx // NX
    x = ctx % NX
    inv_root = 1.0 / math.sqrt(HD)
    scale2 = inv_root * math.log2(math.e)

    def xpeer(dx):
        return lax.rem(x + dx, NX)

    def zpeer(dz):
        return lax.rem(z + dz, NZ)

    def remote(src, dst, ss, rs, dev):
        return pltpu.make_async_remote_copy(
            src_ref=src, dst_ref=dst, send_sem=ss, recv_sem=rs, device_id=dev, device_id_type=MESH
        )

    step = (1, NX - 1)
    back = (NX - 1, 1)
    near = tuple((z * NX + xpeer(d), exp, core) for d in step)
    sent = []

    def go(copy):
        copy.start()
        sent.append(copy)

    partners = list(near)
    for dz in range(0, NZ):
        for dh in range(ND):
            if dz or dh:
                partners.append((zpeer(dz) * NX + x, exp, lax.rem(core + dh, ND)))
    for de in range(1, NE):
        for dh in range(ND):
            partners.append((ctx, lax.rem(exp + de, NE), lax.rem(core + dh, ND)))
    barrier = pltpu.get_barrier_semaphore()
    for partner in partners:
        pl.semaphore_signal(barrier, inc=1, device_id=partner, device_id_type=MESH)
    pl.semaphore_wait(barrier, len(partners))

    kv[x, z, 0:KEYS] = k_ref[...]
    kv[x, z, KEYS : 2 * KEYS] = v_ref[...]
    halves = (pl.ds(0, KEYS), pl.ds(KEYS, KEYS))

    above = tuple((zpeer(d) * NX + x, exp, core) for d in step)

    def kz_copy(way, zz):
        at = kv.at[x, zz]
        return remote(at, at, kz_s.at[way], kz_r.at[way], above[way])

    def kg_copy(way, zz):
        at = kv.at[x, zz, halves[way]]
        return remote(at, at, kg_s.at[way], kg_r.at[way], above[way])

    def kx_copy(way, dz, xx):
        at = kv.at[xx, zpeer(NZ - dz)]
        return remote(at, at, kx_s.at[way * NZ + dz], kx_r.at[way * NZ + dz], near[way])

    def kf_copy(way, dz, xx):
        at = kv.at[xx, zpeer(NZ - dz), halves[way]]
        return remote(at, at, kf_s.at[way * NZ + dz], kf_r.at[way * NZ + dz], near[way])

    for way in range(2):
        go(kz_copy(way, z))
    for way in range(2):
        go(kx_copy(way, 0, x))

    wpad[0:WS] = w_ref[...]
    wpad[WS:WP] = jnp.zeros((WP - WS, FF), BF16)
    w_core = z // 2
    w_slot = lax.rem(z, 2)
    w_here = core == w_core

    def wz_copy(dz):
        return remote(
            wpad,
            wraw.at[w_slot, core],
            wz_s.at[dz],
            wz_r.at[w_slot * 2 + core],
            (zpeer(dz) * NX + x, exp, w_core),
        )


    @pl.when(w_here)
    def _():
        wraw[w_slot, core] = wpad[...]

    @pl.when(jnp.logical_not(w_here))
    def _():
        wz_copy(0).start()

    z_halves = (pl.ds(0, 112), pl.ds(112, WP - 112))

    def wz_wait(s, h):
        remote(wpad, wraw.at[s, h], wz_s.at[0], wz_r.at[s * 2 + h], (ctx, exp, core)).wait_recv()

    def wf_zcopy(way, zz, h):
        at = wraw.at[lax.rem(zz, 2), h, z_halves[way]]
        i = way * 2 + h
        return remote(at, at, wg_s.at[i], wg_r.at[i], above[way])

    w_halves = ((0, WP), (WP, WB - WP))

    def w_rows(xx, s, part=None):
        start = (s * NX + xx) * WB
        if part is None:
            return pl.ds(pl.multiple_of(start, 16), WB)
        return pl.ds(pl.multiple_of(start + w_halves[part][0], 16), w_halves[part][1])

    def wx_copy(way, s, xx):
        at = wfull.at[w_rows(xx, s)]
        return remote(at, at, wx_s.at[way * 2 + s], wx_r.at[way * 2 + s], near[way])

    def wf_copy(way, s, xx):
        at = wfull.at[w_rows(xx, s, way)]
        return remote(at, at, wf_s.at[way * 2 + s], wf_r.at[way * 2 + s], near[way])

    def place_weights(s):
        merged = jnp.concatenate(
            [wraw[s, 0, 0:WS].astype(F32), wraw[s, 1, 0:WS].astype(F32)], axis=0
        )
        wfull[w_rows(x, s)] = merged.astype(BF16)
        for way in range(2):
            wx_copy(way, s, x).start()

    w_other = lax.rem(z + 1, 2)
    w_first = lax.rem(z + (core - w_core) * (core - w_core), 2)

    row_at = lax.broadcasted_iota(jnp.int32, (TOK, TOK), 0)
    col_at = lax.broadcasted_iota(jnp.int32, (TOK, TOK), 1)
    eye = row_at == col_at

    def column(row):
        return jnp.sum(jnp.where(eye, row, 0.0), axis=1, keepdims=True)

    ids_row = ids_ref[...]
    ids_f = ids_row.astype(F32)
    prob_col = column(prob_ref[...].astype(F32))
    same = jnp.where((column(ids_f) == ids_f) & (row_at < col_at), 1.0, 0.0)
    rank = jnp.sum(same, axis=0, keepdims=True).astype(jnp.int32)
    target = ids_row * CAP + rank
    slot_at = lax.broadcasted_iota(jnp.int32, (SLOTS, TOK), 0)
    perm[...] = jnp.where(slot_at == target, 1.0, 0.0).astype(BF16)
    scaled_act = (prob_col * act_ref[...].astype(F32)).astype(BF16)

    def tk_copy(de, dh):
        e_to = lax.rem(exp + de, NE)
        h_to = lax.rem(core + dh, ND)
        i = de * ND + dh
        return remote(
            tsend.at[h_to, e_to],
            trecv.at[core, exp],
            tk_s.at[i],
            tk_r.at[i],
            (ctx, e_to, h_to),
        )

    for half in range(ND):
        base = half * HALF
        first = dot(perm[...], tok_ref[:, base : base + PART])
        second = dot(perm[...], tok_ref[:, base + PART : base + HALF])
        third = dot(perm[...], scaled_act)
        for e in range(NE):
            rows = slice(e * CAP, (e + 1) * CAP)
            tsend[half, e, :, 0 : HALF - PART] = jnp.concatenate(
                [first[rows, 0 : HALF - PART], second[rows]], axis=0
            ).astype(BF16)
            tsend[half, e, :, HALF - PART : PART] = jnp.concatenate(
                [first[rows, HALF - PART : PART], third[rows]], axis=0
            ).astype(BF16)

    @pl.when(w_here)
    def _():
        wz_wait(w_slot, 1 - core)
        place_weights(w_slot)

    for dz in step:
        go(wz_copy(dz))
    trecv[core, exp] = tsend[core, exp]
    go(tk_copy(0, 1))
    for de in (4, 2, 6):
        for dh in range(ND):
            go(tk_copy(de, dh))

    for way in range(2):
        zz = zpeer(back[way])
        kz_copy(way, zz).wait_recv()
        go(kg_copy(way, zz))
        for to in range(2):
            go(kx_copy(to, back[1 - way], x))

    def forward_keys(dz):
        for way in range(2):
            xx = xpeer(back[way])
            kx_copy(way, dz, xx).wait_recv()
            go(kf_copy(way, dz, xx))

    forward_keys(0)
    for way in range(2):
        zz = zpeer(back[way])

        @pl.when(core == zz // 2)
        def _():
            for h in range(ND):
                wz_wait(lax.rem(zz, 2), h)
                wf_zcopy(way, zz, h).start()

    for way in range(2):
        kg_copy(way, zpeer(2)).wait_recv()
    for way in range(2):
        go(kx_copy(way, 2, x))
    forward_keys(1)
    forward_keys(3)
    place_weights(w_other)

    for h in range(GROUP):
        qs[h * QRY : (h + 1) * QRY] = q_ref[:, h * HD : (h + 1) * HD]
        dos[h * QRY : (h + 1) * QRY] = do_ref[:, h * HD : (h + 1) * HD]

    forward_keys(2)

    own_pos = off_ref[ctx] * KEYS + (KEYS - QRY)
    q_pos = own_pos + lax.broadcasted_iota(jnp.int32, (KEYS, QRY), 1)
    k_at = lax.broadcasted_iota(jnp.int32, (KEYS, QRY), 0)
    wide = 2 * QRY

    def bias_of(xx, zz):
        seen = off_ref[zz * NX + xx] * KEYS + k_at <= q_pos
        one = jnp.where(seen, 0.0, NEG_FILL)
        return jnp.concatenate([one, one], axis=1)

    stat_m[...] = jnp.full((1, COLS), NEG_FILL, F32)
    stat_l[...] = jnp.zeros((1, COLS), F32)
    stat_d[...] = jnp.zeros((1, COLS), F32)

    def first_pass(xx, zz):
        bias = bias_of(xx, zz)
        keys = kv[xx, zz, 0:KEYS]
        values = kv[xx, zz, KEYS : 2 * KEYS]
        for g in range(COLS // wide):
            at = slice(g * wide, (g + 1) * wide)
            scores = dot(keys, qs[at], NT) * scale2 + bias
            grads = dot(values, dos[at], NT)
            old = stat_m[:, at]
            peak = jnp.maximum(old, jnp.max(scores, axis=0, keepdims=True))
            shrink = jnp.exp2(old - peak)
            probs = jnp.exp2(scores - peak)
            stat_m[:, at] = peak
            stat_l[:, at] = stat_l[:, at] * shrink + jnp.sum(probs, axis=0, keepdims=True)
            stat_d[:, at] = stat_d[:, at] * shrink + jnp.sum(probs * grads, axis=0, keepdims=True)

    def forward_weights(s):
        for way in range(2):
            xx = xpeer(back[way])
            wx_copy(way, s, xx).wait_recv()
            go(wf_copy(way, s, xx))

    for dx in (0, 1, 3, 2):
        xx = xpeer(dx)
        if dx == 1:
            @pl.when(jnp.logical_not(w_here))
            def _():
                for h in range(ND):
                    for way in range(2):
                        wf_zcopy(way, zpeer(2), h).wait_recv()
                place_weights(w_slot)

            for de in (1, 7, 3, 5):
                for dh in range(ND):
                    go(tk_copy(de, dh))
        if dx == 2:
            for dz in range(NZ):
                for way in range(2):
                    kf_copy(way, dz, xx).wait_recv()

        @pl.loop(0, NZ)
        def _(zz):
            first_pass(xx, zz)

        if dx == 1:
            forward_weights(w_first)
    total = stat_l[...]
    stat_m[...] = stat_m[...] + jnp.log2(total)
    stat_d[...] = stat_d[...] / total
    dq_acc[...] = jnp.zeros((HD, COLS), F32)

    def second_pass(xx, zz):
        bias = bias_of(xx, zz)
        keys = kv[xx, zz, 0:KEYS]
        values = kv[xx, zz, KEYS : 2 * KEYS]
        for g in range(COLS // wide):
            at = slice(g * wide, (g + 1) * wide)
            scores = dot(keys, qs[at], NT) * scale2 + bias
            grads = dot(values, dos[at], NT)
            probs = jnp.exp2(scores - stat_m[:, at])
            p_buf[:, at] = probs.astype(BF16)
            ds_buf[:, at] = (probs * (grads - stat_d[:, at])).astype(BF16)
        dkv[xx, 0, zz] = (dot(ds_buf[...], qs[...]) * inv_root).astype(BF16)
        dkv[xx, 1, zz] = dot(p_buf[...], dos[...]).astype(BF16)
        dq_acc[...] += dot(keys, ds_buf[...], TN)

    def do_copy(way):
        return remote(
            dkv.at[xpeer(2), way], dkv_o.at[way], do_s.at[way], do_r.at[way], near[way]
        )

    def dn_copy(way, part):
        i = way * 2 + part
        return remote(
            dkv.at[xpeer(step[way]), part],
            dkv_n.at[way, part],
            dn_s.at[i],
            dn_r.at[i],
            near[way],
        )

    def pair(h, other, j):
        return (h * 2 + other) * 2 + j, lax.rem(exp + other, 2) + 4 * j

    def unpack(other):
        for de in range(NE):
            for dh in range(ND):
                if (de or dh) and de % 2 == other:
                    tk_copy(de, dh).wait_recv()

        @pl.loop(0, 2 * ND)
        def _(i):
            h = i // 2
            slot, e = pair(h, other, lax.rem(i, 2))
            one = trecv[h, e].astype(F32)
            two = trecv[h, e + 2].astype(F32)
            at = pl.ds(pl.multiple_of(slot * 2 * CAP, 2 * CAP), 2 * CAP)
            gbuf[at, 0:PART] = jnp.concatenate([one[0:CAP], two[0:CAP]], axis=0).astype(BF16)
            rest = jnp.concatenate([one[CAP:], two[CAP:]], axis=0).astype(BF16)
            gbuf[at, PART:HALF] = rest[:, 0 : HALF - PART]
            abuf[at] = rest[:, HALF - PART :]

    g_cols = (pl.ds(0, 3 * HD), pl.ds(3 * HD, FF - 3 * HD))

    def go_copy(way, s, c):
        i = (way * 2 + s) * 2 + c
        return remote(
            wg.at[w_rows(xpeer(2), s, way), g_cols[c]],
            (wg_oa, wg_ob)[way].at[s, :, g_cols[c]],
            go_s.at[i],
            go_r.at[i],
            near[way],
        )

    def gn_copy(way, s, part, c):
        i = ((way * 2 + s) * 2 + part) * 2 + c
        return remote(
            wg.at[w_rows(xpeer(step[way]), s, part), g_cols[c]],
            wg_n.at[way, s, pl.ds(w_halves[part][0], w_halves[part][1]), g_cols[c]],
            gn_s.at[i],
            gn_r.at[i],
            near[way],
        )

    def send_far(s, c):
        for way in range(2):
            go(go_copy(way, s, c))

    def send_near(s, c):
        for way in range(2):
            go(gn_copy(way, s, 1 - way, c))

    def join_grads(s, c):
        for way in range(2):
            go_copy(way, s, c).wait_recv()
            at = w_rows(xpeer(step[way]), s, way)
            theirs = (wg_oa, wg_ob)[way][s, :, g_cols[c]]
            wg[at, g_cols[c]] = (wg[at, g_cols[c]].astype(F32) + theirs.astype(F32)).astype(BF16)
            go(gn_copy(way, s, way, c))

    def weight_grads(chunks):
        for i in chunks:
            at = slice(i * FF, (i + 1) * FF)
            wg[at] = dot(gbuf[:, at], abuf[...], TN).astype(BF16)

    for dx in (2, 1, 3, 0):
        xx = xpeer(dx)
        if dx == 0:
            for way in range(2):
                do_copy(way).wait_recv()
                to = xpeer(step[way])
                dkv[to, way] = (dkv[to, way].astype(F32) + dkv_o[way].astype(F32)).astype(BF16)
                go(dn_copy(way, way))
            unpack(1)
            weight_grads(range(3))
            for c in range(2):
                send_far(0, c)
                send_near(0, c)
            weight_grads(range(3, HALF // FF))

        @pl.loop(0, NZ)
        def _(zz):
            second_pass(xx, zz)

        if dx == 2:
            for way in range(2):
                go(do_copy(way))
            forward_weights(1 - w_first)
        elif dx:
            way = step.index(dx)
            go(dn_copy(way, 1 - way))
            if dx == 1:
                unpack(0)
    join_grads(0, 0)
    join_grads(0, 1)
    send_far(1, 0)
    send_near(1, 0)
    send_far(1, 1)

    def dz_copy(dz):
        return remote(
            dkv_zs.at[zpeer(dz)],
            dkv_zr.at[dz - 1],
            dz_s.at[dz - 1],
            dz_r.at[dz - 1],
            (zpeer(dz) * NX + x, exp, core),
        )

    for way in range(2):
        for part in range(2):
            dn_copy(way, part).wait_recv()

    @pl.loop(0, NZ)
    def _(zz):
        for part in range(2):
            sums = dkv[x, part, zz].astype(F32)
            for way in range(2):
                sums = sums + dkv_n[way, part, zz].astype(F32)
            dkv_zs[zz, part] = sums.astype(BF16)

    for dz in (2, 1, 3):
        go(dz_copy(dz))
    for s in range(2):
        for way in range(2):
            wf_copy(way, s, xpeer(2)).wait_recv()
    hidden = dot(gbuf[...], wfull[...])
    for h in range(ND):
        for other in range(2):
            for j in range(2):
                slot, e = pair(h, other, j)
                for two in range(2):
                    row = (slot * 2 + two) * CAP
                    hsend[h, e + 2 * two] = hidden[row : row + CAP]

    hx_copy = remote(
        hsend.at[1 - core], hother, hx_s.at[0], hx_r.at[0], (ctx, exp, 1 - core)
    )
    go(hx_copy)

    def hb_copy(de):
        e_to = lax.rem(exp + de, NE)
        return remote(hsum.at[e_to], hrecv.at[exp], hb_s.at[de], hb_r.at[de], (ctx, e_to, core))

    join_grads(1, 0)
    send_near(1, 1)


    def gz_copy(s, h, c):
        i = (s * 2 + h) * 2 + c
        return remote(
            wg_zs.at[s, h, :, g_cols[c]],
            wg_zr.at[z, :, g_cols[c]],
            gz_s.at[i],
            gz_r.at[z * 2 + c],
            ((2 * core + s) * NX + x, exp, h),
        )

    def sum_grads(s, c):
        for way in range(2):
            for part in range(2):
                gn_copy(way, s, part, c).wait_recv()
        sums = wg[w_rows(x, s), g_cols[c]].astype(F32)
        for way in range(2):
            sums = sums + wg_n[way, s, :, g_cols[c]].astype(F32)
        for h in range(ND):
            wg_zs[s, h, 0:WS, g_cols[c]] = sums[h * WS : (h + 1) * WS].astype(BF16)
            own = (2 * core + s == z) & (core == h)

            @pl.when(own)
            def _():
                wg_zr[z, :, g_cols[c]] = wg_zs[s, h, :, g_cols[c]]

            @pl.when(jnp.logical_not(own))
            def _():
                gz_copy(s, h, c).start()

    wg_zs[:, :, WS:WP] = jnp.zeros((2, ND, WP - WS, FF), BF16)
    sum_grads(0, 0)
    sum_grads(0, 1)
    hx_copy.wait_recv()
    hsum[...] = hsend[core] + hother[...]
    hrecv[exp] = hsum[exp]
    for de in (1, 7, 3, 5, 4, 2, 6):
        go(hb_copy(de))
    join_grads(1, 1)
    sum_grads(1, 0)
    sum_grads(1, 1)
    for h in range(GROUP):
        dq_out[:, h * HD : (h + 1) * HD] = (
            jnp.transpose(dq_acc[:, h * QRY : (h + 1) * QRY]) * inv_root
        ).astype(BF16)

    for de in range(1, NE):
        hb_copy(de).wait_recv()
    back_rows = jnp.concatenate([hrecv[e] for e in range(NE)], axis=0)
    high = back_rows.astype(BF16)
    low = (back_rows - high.astype(F32)).astype(BF16)
    mine = dot(perm[...], high, TN) + dot(perm[...], low, TN)
    hid_out[...] = (prob_col * mine).astype(BF16)
    route = jnp.sum(act_ref[...].astype(F32) * mine, axis=1, keepdims=True)
    route_out[...] = jnp.sum(jnp.where(eye, route, 0.0), axis=0, keepdims=True).astype(BF16)

    for dz in range(1, NZ):
        dz_copy(dz).wait_recv()
    for part, out in enumerate((dk_out, dv_out)):
        sums = dkv_zs[z, part].astype(F32)
        for i in range(NZ - 1):
            sums = sums + dkv_zr[i, part].astype(F32)
        out[...] = sums.astype(BF16)

    for c in range(2):
        for zz in range(NZ):

            @pl.when(jnp.logical_not((zz == z) & (core == w_core)))
            def _():
                remote(
                    wg_zs.at[0, 0, :, g_cols[c]],
                    wg_zr.at[zz, :, g_cols[c]],
                    gz_s.at[0],
                    gz_r.at[zz * 2 + c],
                    (ctx, exp, core),
                ).wait_recv()

        sums = wg_zr[0, :, g_cols[c]].astype(F32)
        for zz in range(1, NZ):
            sums = sums + wg_zr[zz, :, g_cols[c]].astype(F32)
        dw_out[:, g_cols[c]] = sums[0:WS].astype(BF16)

    for copy in sent:
        copy.wait_send()
    for way in range(2):
        for s in range(2):
            wx_copy(way, s, x).wait_send()

    @pl.when(jnp.logical_not(w_here))
    def _():
        wz_copy(0).wait_send()

    for way in range(2):
        zz = zpeer(back[way])

        @pl.when(core == zz // 2)
        def _():
            for h in range(ND):
                wf_zcopy(way, zz, h).wait_send()

    for s in range(2):
        for h in range(ND):

            @pl.when(jnp.logical_not((2 * core + s == z) & (core == h)))
            def _():
                for c in range(2):
                    gz_copy(s, h, c).wait_send()


def finish(*refs):
    count = len(refs) // 2
    for source, out in zip(refs[:count], refs[count:]):
        out[...] = source[...]


def per_device(
    query,
    key_rows,
    value_rows,
    out_grad,
    block_offsets,
    tok_grad,
    hidden_act,
    router_prob,
    expert_ids,
    down_weight,
):
    vmem = pl.BlockSpec(memory_space=pltpu.VMEM)
    smem = pl.BlockSpec(memory_space=pltpu.SMEM)
    dma = pltpu.SemaphoreType.DMA
    scratch = [
        pltpu.VMEM((NX, NZ, 2 * KEYS, HD), BF16),
        pltpu.VMEM((COLS, HD), BF16),
        pltpu.VMEM((COLS, HD), BF16),
        pltpu.VMEM((1, COLS), F32),
        pltpu.VMEM((1, COLS), F32),
        pltpu.VMEM((1, COLS), F32),
        pltpu.VMEM((KEYS, COLS), BF16),
        pltpu.VMEM((KEYS, COLS), BF16),
        pltpu.VMEM((HD, COLS), F32),
        pltpu.VMEM((NX, 2, NZ, KEYS, HD), BF16),
        pltpu.VMEM((2, NZ, KEYS, HD), BF16),
        pltpu.VMEM((2, 2, NZ, KEYS, HD), BF16),
        pltpu.VMEM((NZ, 2, KEYS, HD), BF16),
        pltpu.VMEM((NZ - 1, 2, KEYS, HD), BF16),
        pltpu.VMEM((SLOTS, TOK), BF16),
        pltpu.VMEM((ND, NE, 2 * CAP, PART), BF16),
        pltpu.VMEM((ND, NE, 2 * CAP, PART), BF16),
        pltpu.VMEM((ROWS, HALF), BF16),
        pltpu.VMEM((ROWS, FF), BF16),
        pltpu.VMEM((WP, FF), BF16),
        pltpu.VMEM((2, ND, WP, FF), BF16),
        pltpu.VMEM((HALF, FF), BF16),
        pltpu.VMEM((HALF, FF), BF16),
        pltpu.VMEM((2, WP, FF), BF16),
        pltpu.VMEM((2, WB - WP, FF), BF16),
        pltpu.VMEM((2, 2, WB, FF), BF16),
        pltpu.VMEM((2, ND, WP, FF), BF16),
        pltpu.VMEM((NZ, WP, FF), BF16),
        pltpu.VMEM((ND, NE, CAP, FF), F32),
        pltpu.VMEM((NE, CAP, FF), F32),
        pltpu.VMEM((NE, CAP, FF), F32),
        pltpu.VMEM((NE, CAP, FF), F32),
    ]
    for size in (
        2,
        2,
        2 * NZ,
        2 * NZ,
        NZ,
        4,
        4,
        4,
        NE * ND,
        2,
        4,
        NZ - 1,
        8,
        16,
        8,
        1,
        NE,
    ):
        scratch += [dma((size,)), dma((size,))]
    shapes = (
        jax.ShapeDtypeStruct((QRY, GROUP * HD), BF16),
        jax.ShapeDtypeStruct((KEYS, HD), BF16),
        jax.ShapeDtypeStruct((KEYS, HD), BF16),
        jax.ShapeDtypeStruct((TOK, FF), BF16),
        jax.ShapeDtypeStruct((1, TOK), BF16),
        jax.ShapeDtypeStruct((WS, FF), BF16),
    )
    results = pl.pallas_call(
        kernel,
        name="layer_backward",
        out_shape=shapes,
        in_specs=[smem] + [vmem] * 9,
        out_specs=[vmem] * 6,
        scratch_shapes=scratch,
        compiler_params=pltpu.CompilerParams(
            collective_id=0, has_side_effects=True, vmem_limit_bytes=60 << 20
        ),
    )(
        block_offsets,
        query[0],
        key_rows[0],
        value_rows[0],
        out_grad[0],
        tok_grad,
        hidden_act,
        router_prob.reshape(1, TOK),
        expert_ids.reshape(1, TOK),
        down_weight[0],
    )
    dq, dk, dv, hidden, route, dw = pl.pallas_call(
        finish, name="finish", out_shape=shapes, in_specs=[vmem] * 6, out_specs=[vmem] * 6
    )(*results)
    return (dq[None], dk[None], dv[None], hidden, route[0], dw[None])


def solution(mesh):
    in_specs = (
        P("dp", "ctx", "exp"),
        P("dp", "ctx", "exp"),
        P("dp", "ctx", "exp"),
        P("dp", "ctx", "exp"),
        P(),
        P(("ctx", "exp", "dp"), None),
        P(("ctx", "exp", "dp"), None),
        P(("ctx", "exp", "dp")),
        P(("ctx", "exp", "dp"), None),
        P("exp", ("ctx", "dp"), None),
    )
    out_specs = (
        P("dp", "ctx", "exp"),
        P("dp", "ctx", "exp"),
        P("dp", "ctx", "exp"),
        P(("ctx", "exp", "dp"), None),
        P(("ctx", "exp", "dp")),
        P("exp", ("ctx", "dp"), None),
    )
    return jax.shard_map(
        per_device, mesh=mesh, in_specs=in_specs, out_specs=out_specs, check_vma=False
    )
```

```python
import math

import jax
import jax.numpy as jnp
from jax import lax
from jax.experimental import pallas as pl
from jax.experimental.pallas import tpu as pltpu
from jax.sharding import PartitionSpec as P

HD = 128
GROUP = 10
NEG_FILL = -1e30
MESH = pl.DeviceIdType.MESH
F32 = jnp.float32
BF16 = jnp.bfloat16

NX, NZ, NE, ND = 4, 4, 8, 2
KEYS = 256
QRY = 128
COLS = GROUP * QRY
TOK = 128
CAP = 24
D = 6400
HALF = D // 2
FF = 640
PART = (HALF + FF) // 2
WB = 400
WS = 200
WP = 208
SLOTS = NE * CAP
ROWS = ND * SLOTS

NT = (((1,), (1,)), ((), ()))
TN = (((0,), (0,)), ((), ()))


def dot(a, b, dims=(((1,), (0,)), ((), ()))):
    return lax.dot_general(a, b, dims, preferred_element_type=F32)


def kernel(
    off_ref,
    q_ref,
    k_ref,
    v_ref,
    do_ref,
    tok_ref,
    act_ref,
    prob_ref,
    ids_ref,
    w_ref,
    dq_out,
    dk_out,
    dv_out,
    hid_out,
    route_out,
    dw_out,
    kv,
    qs,
    dos,
    stat_m,
    stat_l,
    stat_d,
    p_buf,
    ds_buf,
    dq_acc,
    dkv,
    dkv_o,
    dkv_n,
    dkv_zs,
    dkv_zr,
    perm,
    tsend,
    trecv,
    gbuf,
    abuf,
    wpad,
    wraw,
    wfull,
    wg,
    wg_oa,
    wg_ob,
    wg_n,
    wg_zs,
    wg_zr,
    hsend,
    hother,
    hsum,
    hrecv,
    kz_s,
    kz_r,
    kg_s,
    kg_r,
    kx_s,
    kx_r,
    kf_s,
    kf_r,
    wz_s,
    wz_r,
    wg_s,
    wg_r,
    wx_s,
    wx_r,
    wf_s,
    wf_r,
    tk_s,
    tk_r,
    do_s,
    do_r,
    dn_s,
    dn_r,
    dz_s,
    dz_r,
    go_s,
    go_r,
    gn_s,
    gn_r,
    gz_s,
    gz_r,
    hx_s,
    hx_r,
    hb_s,
    hb_r,
):
    ctx = lax.axis_index("ctx")
    exp = lax.axis_index("exp")
    core = lax.axis_index("dp")
    z = ctx // NX
    x = ctx % NX
    inv_root = 1.0 / math.sqrt(HD)
    scale2 = inv_root * math.log2(math.e)

    def xpeer(dx):
        return lax.rem(x + dx, NX)

    def zpeer(dz):
        return lax.rem(z + dz, NZ)

    def remote(src, dst, ss, rs, dev):
        return pltpu.make_async_remote_copy(
            src_ref=src, dst_ref=dst, send_sem=ss, recv_sem=rs, device_id=dev, device_id_type=MESH
        )

    step = (1, NX - 1)
    back = (NX - 1, 1)
    near = tuple((z * NX + xpeer(d), exp, core) for d in step)
    sent = []

    def go(copy):
        copy.start()
        sent.append(copy)

    partners = list(near)
    for dz in range(0, NZ):
        for dh in range(ND):
            if dz or dh:
                partners.append((zpeer(dz) * NX + x, exp, lax.rem(core + dh, ND)))
    for de in range(1, NE):
        for dh in range(ND):
            partners.append((ctx, lax.rem(exp + de, NE), lax.rem(core + dh, ND)))
    barrier = pltpu.get_barrier_semaphore()
    for partner in partners:
        pl.semaphore_signal(barrier, inc=1, device_id=partner, device_id_type=MESH)
    pl.semaphore_wait(barrier, len(partners))

    kv[x, z, 0:KEYS] = k_ref[...]
    kv[x, z, KEYS : 2 * KEYS] = v_ref[...]
    halves = (pl.ds(0, KEYS), pl.ds(KEYS, KEYS))

    above = tuple((zpeer(d) * NX + x, exp, core) for d in step)

    def kz_copy(way, zz):
        at = kv.at[x, zz]
        return remote(at, at, kz_s.at[way], kz_r.at[way], above[way])

    def kg_copy(way, zz):
        at = kv.at[x, zz, halves[way]]
        return remote(at, at, kg_s.at[way], kg_r.at[way], above[way])

    def kx_copy(way, dz, xx):
        at = kv.at[xx, zpeer(NZ - dz)]
        return remote(at, at, kx_s.at[way * NZ + dz], kx_r.at[way * NZ + dz], near[way])

    def kf_copy(way, dz, xx):
        at = kv.at[xx, zpeer(NZ - dz), halves[way]]
        return remote(at, at, kf_s.at[way * NZ + dz], kf_r.at[way * NZ + dz], near[way])

    for way in range(2):
        go(kz_copy(way, z))
    for way in range(2):
        go(kx_copy(way, 0, x))

    wpad[0:WS] = w_ref[...]
    wpad[WS:WP] = jnp.zeros((WP - WS, FF), BF16)
    w_core = z // 2
    w_slot = lax.rem(z, 2)
    w_here = core == w_core

    def wz_copy(dz):
        return remote(
            wpad,
            wraw.at[w_slot, core],
            wz_s.at[dz],
            wz_r.at[w_slot * 2 + core],
            (zpeer(dz) * NX + x, exp, w_core),
        )


    @pl.when(w_here)
    def _():
        wraw[w_slot, core] = wpad[...]

    @pl.when(jnp.logical_not(w_here))
    def _():
        wz_copy(0).start()

    z_halves = (pl.ds(0, 112), pl.ds(112, WP - 112))

    def wz_wait(s, h):
        remote(wpad, wraw.at[s, h], wz_s.at[0], wz_r.at[s * 2 + h], (ctx, exp, core)).wait_recv()

    def wf_zcopy(way, zz, h):
        at = wraw.at[lax.rem(zz, 2), h, z_halves[way]]
        i = way * 2 + h
        return remote(at, at, wg_s.at[i], wg_r.at[i], above[way])

    w_halves = ((0, WP), (WP, WB - WP))

    def w_rows(xx, s, part=None):
        start = (s * NX + xx) * WB
        if part is None:
            return pl.ds(pl.multiple_of(start, 16), WB)
        return pl.ds(pl.multiple_of(start + w_halves[part][0], 16), w_halves[part][1])

    def wx_copy(way, s, xx):
        at = wfull.at[w_rows(xx, s)]
        return remote(at, at, wx_s.at[way * 2 + s], wx_r.at[way * 2 + s], near[way])

    def wf_copy(way, s, xx):
        at = wfull.at[w_rows(xx, s, way)]
        return remote(at, at, wf_s.at[way * 2 + s], wf_r.at[way * 2 + s], near[way])

    def place_weights(s):
        merged = jnp.concatenate(
            [wraw[s, 0, 0:WS].astype(F32), wraw[s, 1, 0:WS].astype(F32)], axis=0
        )
        wfull[w_rows(x, s)] = merged.astype(BF16)
        for way in range(2):
            wx_copy(way, s, x).start()

    w_other = lax.rem(z + 1, 2)
    w_first = lax.rem(z + (core - w_core) * (core - w_core), 2)

    @pl.when(w_here)
    def _():
        wz_wait(w_slot, 1 - core)
        place_weights(w_slot)

    for dz in step:
        go(wz_copy(dz))
    for way in range(2):
        zz = zpeer(back[way])
        kz_copy(way, zz).wait_recv()
        go(kg_copy(way, zz))
        for to in range(2):
            go(kx_copy(to, back[1 - way], x))

    def forward_keys(dz):
        for way in range(2):
            xx = xpeer(back[way])
            kx_copy(way, dz, xx).wait_recv()
            go(kf_copy(way, dz, xx))

    forward_keys(0)
    for way in range(2):
        zz = zpeer(back[way])

        @pl.when(core == zz // 2)
        def _():
            for h in range(ND):
                wz_wait(lax.rem(zz, 2), h)
                wf_zcopy(way, zz, h).start()

    for way in range(2):
        kg_copy(way, zpeer(2)).wait_recv()
    for way in range(2):
        go(kx_copy(way, 2, x))
    forward_keys(1)
    forward_keys(3)
    place_weights(w_other)

    row_at = lax.broadcasted_iota(jnp.int32, (TOK, TOK), 0)
    col_at = lax.broadcasted_iota(jnp.int32, (TOK, TOK), 1)
    eye = row_at == col_at

    def column(row):
        return jnp.sum(jnp.where(eye, row, 0.0), axis=1, keepdims=True)

    ids_row = ids_ref[...]
    ids_f = ids_row.astype(F32)
    prob_col = column(prob_ref[...].astype(F32))
    same = jnp.where((column(ids_f) == ids_f) & (row_at < col_at), 1.0, 0.0)
    rank = jnp.sum(same, axis=0, keepdims=True).astype(jnp.int32)
    target = ids_row * CAP + rank
    slot_at = lax.broadcasted_iota(jnp.int32, (SLOTS, TOK), 0)
    perm[...] = jnp.where(slot_at == target, 1.0, 0.0).astype(BF16)
    scaled_act = (prob_col * act_ref[...].astype(F32)).astype(BF16)

    def tk_copy(de, dh):
        e_to = lax.rem(exp + de, NE)
        h_to = lax.rem(core + dh, ND)
        i = de * ND + dh
        return remote(
            tsend.at[h_to, e_to],
            trecv.at[core, exp],
            tk_s.at[i],
            tk_r.at[i],
            (ctx, e_to, h_to),
        )

    for half in range(ND):
        base = half * HALF
        first = dot(perm[...], tok_ref[:, base : base + PART])
        second = dot(perm[...], tok_ref[:, base + PART : base + HALF])
        third = dot(perm[...], scaled_act)
        for e in range(NE):
            rows = slice(e * CAP, (e + 1) * CAP)
            tsend[half, e, :, 0 : HALF - PART] = jnp.concatenate(
                [first[rows, 0 : HALF - PART], second[rows]], axis=0
            ).astype(BF16)
            tsend[half, e, :, HALF - PART : PART] = jnp.concatenate(
                [first[rows, HALF - PART : PART], third[rows]], axis=0
            ).astype(BF16)

    trecv[core, exp] = tsend[core, exp]
    go(tk_copy(0, 1))
    for de in (4, 2, 6):
        for dh in range(ND):
            go(tk_copy(de, dh))


    for h in range(GROUP):
        qs[h * QRY : (h + 1) * QRY] = q_ref[:, h * HD : (h + 1) * HD]
        dos[h * QRY : (h + 1) * QRY] = do_ref[:, h * HD : (h + 1) * HD]

    forward_keys(2)

    own_pos = off_ref[ctx] * KEYS + (KEYS - QRY)
    q_pos = own_pos + lax.broadcasted_iota(jnp.int32, (KEYS, QRY), 1)
    k_at = lax.broadcasted_iota(jnp.int32, (KEYS, QRY), 0)
    wide = 2 * QRY

    def bias_of(xx, zz):
        seen = off_ref[zz * NX + xx] * KEYS + k_at <= q_pos
        one = jnp.where(seen, 0.0, NEG_FILL)
        return jnp.concatenate([one, one], axis=1)

    stat_m[...] = jnp.full((1, COLS), NEG_FILL, F32)
    stat_l[...] = jnp.zeros((1, COLS), F32)
    stat_d[...] = jnp.zeros((1, COLS), F32)

    def first_pass(xx, zz):
        bias = bias_of(xx, zz)
        keys = kv[xx, zz, 0:KEYS]
        values = kv[xx, zz, KEYS : 2 * KEYS]
        for g in range(COLS // wide):
            at = slice(g * wide, (g + 1) * wide)
            scores = dot(keys, qs[at], NT) * scale2 + bias
            grads = dot(values, dos[at], NT)
            old = stat_m[:, at]
            peak = jnp.maximum(old, jnp.max(scores, axis=0, keepdims=True))
            shrink = jnp.exp2(old - peak)
            probs = jnp.exp2(scores - peak)
            stat_m[:, at] = peak
            stat_l[:, at] = stat_l[:, at] * shrink + jnp.sum(probs, axis=0, keepdims=True)
            stat_d[:, at] = stat_d[:, at] * shrink + jnp.sum(probs * grads, axis=0, keepdims=True)

    def forward_weights(s):
        for way in range(2):
            xx = xpeer(back[way])
            wx_copy(way, s, xx).wait_recv()
            go(wf_copy(way, s, xx))

    for dx in (0, 1, 3, 2):
        xx = xpeer(dx)
        if dx == 1:
            @pl.when(jnp.logical_not(w_here))
            def _():
                for h in range(ND):
                    for way in range(2):
                        wf_zcopy(way, zpeer(2), h).wait_recv()
                place_weights(w_slot)

            for de in (1, 7, 3, 5):
                for dh in range(ND):
                    go(tk_copy(de, dh))
        if dx == 2:
            for dz in range(NZ):
                for way in range(2):
                    kf_copy(way, dz, xx).wait_recv()

        @pl.loop(0, NZ)
        def _(zz):
            first_pass(xx, zz)

        if dx == 1:
            forward_weights(w_first)
    total = stat_l[...]
    stat_m[...] = stat_m[...] + jnp.log2(total)
    stat_d[...] = stat_d[...] / total
    dq_acc[...] = jnp.zeros((HD, COLS), F32)

    def second_pass(xx, zz):
        bias = bias_of(xx, zz)
        keys = kv[xx, zz, 0:KEYS]
        values = kv[xx, zz, KEYS : 2 * KEYS]
        for g in range(COLS // wide):
            at = slice(g * wide, (g + 1) * wide)
            scores = dot(keys, qs[at], NT) * scale2 + bias
            grads = dot(values, dos[at], NT)
            probs = jnp.exp2(scores - stat_m[:, at])
            p_buf[:, at] = probs.astype(BF16)
            ds_buf[:, at] = (probs * (grads - stat_d[:, at])).astype(BF16)
        dkv[xx, 0, zz] = (dot(ds_buf[...], qs[...]) * inv_root).astype(BF16)
        dkv[xx, 1, zz] = dot(p_buf[...], dos[...]).astype(BF16)
        dq_acc[...] += dot(keys, ds_buf[...], TN)

    def do_copy(way):
        return remote(
            dkv.at[xpeer(2), way], dkv_o.at[way], do_s.at[way], do_r.at[way], near[way]
        )

    def dn_copy(way, part):
        i = way * 2 + part
        return remote(
            dkv.at[xpeer(step[way]), part],
            dkv_n.at[way, part],
            dn_s.at[i],
            dn_r.at[i],
            near[way],
        )

    def pair(h, other, j):
        return (h * 2 + other) * 2 + j, lax.rem(exp + other, 2) + 4 * j

    def unpack(other):
        for de in range(NE):
            for dh in range(ND):
                if (de or dh) and de % 2 == other:
                    tk_copy(de, dh).wait_recv()

        @pl.loop(0, 2 * ND)
        def _(i):
            h = i // 2
            slot, e = pair(h, other, lax.rem(i, 2))
            one = trecv[h, e].astype(F32)
            two = trecv[h, e + 2].astype(F32)
            at = pl.ds(pl.multiple_of(slot * 2 * CAP, 2 * CAP), 2 * CAP)
            gbuf[at, 0:PART] = jnp.concatenate([one[0:CAP], two[0:CAP]], axis=0).astype(BF16)
            rest = jnp.concatenate([one[CAP:], two[CAP:]], axis=0).astype(BF16)
            gbuf[at, PART:HALF] = rest[:, 0 : HALF - PART]
            abuf[at] = rest[:, HALF - PART :]

    g_cols = (pl.ds(0, 3 * HD), pl.ds(3 * HD, FF - 3 * HD))

    def go_copy(way, s, c):
        i = (way * 2 + s) * 2 + c
        return remote(
            wg.at[w_rows(xpeer(2), s, way), g_cols[c]],
            (wg_oa, wg_ob)[way].at[s, :, g_cols[c]],
            go_s.at[i],
            go_r.at[i],
            near[way],
        )

    def gn_copy(way, s, part, c):
        i = ((way * 2 + s) * 2 + part) * 2 + c
        return remote(
            wg.at[w_rows(xpeer(step[way]), s, part), g_cols[c]],
            wg_n.at[way, s, pl.ds(w_halves[part][0], w_halves[part][1]), g_cols[c]],
            gn_s.at[i],
            gn_r.at[i],
            near[way],
        )

    def send_far(s, c):
        for way in range(2):
            go(go_copy(way, s, c))

    def send_near(s, c):
        for way in range(2):
            go(gn_copy(way, s, 1 - way, c))

    def join_grads(s, c):
        for way in range(2):
            go_copy(way, s, c).wait_recv()
            at = w_rows(xpeer(step[way]), s, way)
            theirs = (wg_oa, wg_ob)[way][s, :, g_cols[c]]
            wg[at, g_cols[c]] = (wg[at, g_cols[c]].astype(F32) + theirs.astype(F32)).astype(BF16)
            go(gn_copy(way, s, way, c))

    def weight_grads(chunks):
        for i in chunks:
            at = slice(i * FF, (i + 1) * FF)
            wg[at] = dot(gbuf[:, at], abuf[...], TN).astype(BF16)

    for dx in (2, 1, 3, 0):
        xx = xpeer(dx)
        if dx == 0:
            for way in range(2):
                do_copy(way).wait_recv()
                to = xpeer(step[way])
                dkv[to, way] = (dkv[to, way].astype(F32) + dkv_o[way].astype(F32)).astype(BF16)
                go(dn_copy(way, way))
            unpack(1)
            weight_grads(range(3))
            for c in range(2):
                send_far(0, c)
                send_near(0, c)
            weight_grads(range(3, HALF // FF))

        @pl.loop(0, NZ)
        def _(zz):
            second_pass(xx, zz)

        if dx == 2:
            for way in range(2):
                go(do_copy(way))
            forward_weights(1 - w_first)
        elif dx:
            way = step.index(dx)
            go(dn_copy(way, 1 - way))
            if dx == 1:
                unpack(0)
    join_grads(0, 0)
    join_grads(0, 1)
    send_far(1, 0)
    send_near(1, 0)
    send_far(1, 1)

    def dz_copy(dz):
        return remote(
            dkv_zs.at[zpeer(dz)],
            dkv_zr.at[dz - 1],
            dz_s.at[dz - 1],
            dz_r.at[dz - 1],
            (zpeer(dz) * NX + x, exp, core),
        )

    for way in range(2):
        for part in range(2):
            dn_copy(way, part).wait_recv()

    @pl.loop(0, NZ)
    def _(zz):
        for part in range(2):
            sums = dkv[x, part, zz].astype(F32)
            for way in range(2):
                sums = sums + dkv_n[way, part, zz].astype(F32)
            dkv_zs[zz, part] = sums.astype(BF16)

    for dz in (2, 1, 3):
        go(dz_copy(dz))
    for s in range(2):
        for way in range(2):
            wf_copy(way, s, xpeer(2)).wait_recv()
    hidden = dot(gbuf[...], wfull[...])
    for h in range(ND):
        for other in range(2):
            for j in range(2):
                slot, e = pair(h, other, j)
                for two in range(2):
                    row = (slot * 2 + two) * CAP
                    hsend[h, e + 2 * two] = hidden[row : row + CAP]

    hx_copy = remote(
        hsend.at[1 - core], hother, hx_s.at[0], hx_r.at[0], (ctx, exp, 1 - core)
    )
    go(hx_copy)

    def hb_copy(de):
        e_to = lax.rem(exp + de, NE)
        return remote(hsum.at[e_to], hrecv.at[exp], hb_s.at[de], hb_r.at[de], (ctx, e_to, core))

    join_grads(1, 0)
    send_near(1, 1)


    def gz_copy(s, h, c):
        i = (s * 2 + h) * 2 + c
        return remote(
            wg_zs.at[s, h, :, g_cols[c]],
            wg_zr.at[z, :, g_cols[c]],
            gz_s.at[i],
            gz_r.at[z * 2 + c],
            ((2 * core + s) * NX + x, exp, h),
        )

    def sum_grads(s, c):
        for way in range(2):
            for part in range(2):
                gn_copy(way, s, part, c).wait_recv()
        sums = wg[w_rows(x, s), g_cols[c]].astype(F32)
        for way in range(2):
            sums = sums + wg_n[way, s, :, g_cols[c]].astype(F32)
        for h in range(ND):
            wg_zs[s, h, 0:WS, g_cols[c]] = sums[h * WS : (h + 1) * WS].astype(BF16)
            own = (2 * core + s == z) & (core == h)

            @pl.when(own)
            def _():
                wg_zr[z, :, g_cols[c]] = wg_zs[s, h, :, g_cols[c]]

            @pl.when(jnp.logical_not(own))
            def _():
                gz_copy(s, h, c).start()

    wg_zs[:, :, WS:WP] = jnp.zeros((2, ND, WP - WS, FF), BF16)
    sum_grads(0, 0)
    sum_grads(0, 1)
    hx_copy.wait_recv()
    hsum[...] = hsend[core] + hother[...]
    hrecv[exp] = hsum[exp]
    for de in (1, 7, 3, 5, 4, 2, 6):
        go(hb_copy(de))
    join_grads(1, 1)
    sum_grads(1, 0)
    sum_grads(1, 1)
    for h in range(GROUP):
        dq_out[:, h * HD : (h + 1) * HD] = (
            jnp.transpose(dq_acc[:, h * QRY : (h + 1) * QRY]) * inv_root
        ).astype(BF16)

    for de in range(1, NE):
        hb_copy(de).wait_recv()
    back_rows = jnp.concatenate([hrecv[e] for e in range(NE)], axis=0)
    high = back_rows.astype(BF16)
    low = (back_rows - high.astype(F32)).astype(BF16)
    mine = dot(perm[...], high, TN) + dot(perm[...], low, TN)
    hid_out[...] = (prob_col * mine).astype(BF16)
    route = jnp.sum(act_ref[...].astype(F32) * mine, axis=1, keepdims=True)
    route_out[...] = jnp.sum(jnp.where(eye, route, 0.0), axis=0, keepdims=True).astype(BF16)

    for dz in range(1, NZ):
        dz_copy(dz).wait_recv()
    for part, out in enumerate((dk_out, dv_out)):
        sums = dkv_zs[z, part].astype(F32)
        for i in range(NZ - 1):
            sums = sums + dkv_zr[i, part].astype(F32)
        out[...] = sums.astype(BF16)

    for c in range(2):
        for zz in range(NZ):

            @pl.when(jnp.logical_not((zz == z) & (core == w_core)))
            def _():
                remote(
                    wg_zs.at[0, 0, :, g_cols[c]],
                    wg_zr.at[zz, :, g_cols[c]],
                    gz_s.at[0],
                    gz_r.at[zz * 2 + c],
                    (ctx, exp, core),
                ).wait_recv()

        sums = wg_zr[0, :, g_cols[c]].astype(F32)
        for zz in range(1, NZ):
            sums = sums + wg_zr[zz, :, g_cols[c]].astype(F32)
        dw_out[:, g_cols[c]] = sums[0:WS].astype(BF16)

    for copy in sent:
        copy.wait_send()
    for way in range(2):
        for s in range(2):
            wx_copy(way, s, x).wait_send()

    @pl.when(jnp.logical_not(w_here))
    def _():
        wz_copy(0).wait_send()

    for way in range(2):
        zz = zpeer(back[way])

        @pl.when(core == zz // 2)
        def _():
            for h in range(ND):
                wf_zcopy(way, zz, h).wait_send()

    for s in range(2):
        for h in range(ND):

            @pl.when(jnp.logical_not((2 * core + s == z) & (core == h)))
            def _():
                for c in range(2):
                    gz_copy(s, h, c).wait_send()


def finish(*refs):
    count = len(refs) // 2
    for source, out in zip(refs[:count], refs[count:]):
        out[...] = source[...]


def per_device(
    query,
    key_rows,
    value_rows,
    out_grad,
    block_offsets,
    tok_grad,
    hidden_act,
    router_prob,
    expert_ids,
    down_weight,
):
    vmem = pl.BlockSpec(memory_space=pltpu.VMEM)
    smem = pl.BlockSpec(memory_space=pltpu.SMEM)
    dma = pltpu.SemaphoreType.DMA
    scratch = [
        pltpu.VMEM((NX, NZ, 2 * KEYS, HD), BF16),
        pltpu.VMEM((COLS, HD), BF16),
        pltpu.VMEM((COLS, HD), BF16),
        pltpu.VMEM((1, COLS), F32),
        pltpu.VMEM((1, COLS), F32),
        pltpu.VMEM((1, COLS), F32),
        pltpu.VMEM((KEYS, COLS), BF16),
        pltpu.VMEM((KEYS, COLS), BF16),
        pltpu.VMEM((HD, COLS), F32),
        pltpu.VMEM((NX, 2, NZ, KEYS, HD), BF16),
        pltpu.VMEM((2, NZ, KEYS, HD), BF16),
        pltpu.VMEM((2, 2, NZ, KEYS, HD), BF16),
        pltpu.VMEM((NZ, 2, KEYS, HD), BF16),
        pltpu.VMEM((NZ - 1, 2, KEYS, HD), BF16),
        pltpu.VMEM((SLOTS, TOK), BF16),
        pltpu.VMEM((ND, NE, 2 * CAP, PART), BF16),
        pltpu.VMEM((ND, NE, 2 * CAP, PART), BF16),
        pltpu.VMEM((ROWS, HALF), BF16),
        pltpu.VMEM((ROWS, FF), BF16),
        pltpu.VMEM((WP, FF), BF16),
        pltpu.VMEM((2, ND, WP, FF), BF16),
        pltpu.VMEM((HALF, FF), BF16),
        pltpu.VMEM((HALF, FF), BF16),
        pltpu.VMEM((2, WP, FF), BF16),
        pltpu.VMEM((2, WB - WP, FF), BF16),
        pltpu.VMEM((2, 2, WB, FF), BF16),
        pltpu.VMEM((2, ND, WP, FF), BF16),
        pltpu.VMEM((NZ, WP, FF), BF16),
        pltpu.VMEM((ND, NE, CAP, FF), F32),
        pltpu.VMEM((NE, CAP, FF), F32),
        pltpu.VMEM((NE, CAP, FF), F32),
        pltpu.VMEM((NE, CAP, FF), F32),
    ]
    for size in (
        2,
        2,
        2 * NZ,
        2 * NZ,
        NZ,
        4,
        4,
        4,
        NE * ND,
        2,
        4,
        NZ - 1,
        8,
        16,
        8,
        1,
        NE,
    ):
        scratch += [dma((size,)), dma((size,))]
    shapes = (
        jax.ShapeDtypeStruct((QRY, GROUP * HD), BF16),
        jax.ShapeDtypeStruct((KEYS, HD), BF16),
        jax.ShapeDtypeStruct((KEYS, HD), BF16),
        jax.ShapeDtypeStruct((TOK, FF), BF16),
        jax.ShapeDtypeStruct((1, TOK), BF16),
        jax.ShapeDtypeStruct((WS, FF), BF16),
    )
    results = pl.pallas_call(
        kernel,
        name="layer_backward",
        out_shape=shapes,
        in_specs=[smem] + [vmem] * 9,
        out_specs=[vmem] * 6,
        scratch_shapes=scratch,
        compiler_params=pltpu.CompilerParams(
            collective_id=0, has_side_effects=True, vmem_limit_bytes=60 << 20
        ),
    )(
        block_offsets,
        query[0],
        key_rows[0],
        value_rows[0],
        out_grad[0],
        tok_grad,
        hidden_act,
        router_prob.reshape(1, TOK),
        expert_ids.reshape(1, TOK),
        down_weight[0],
    )
    dq, dk, dv, hidden, route, dw = pl.pallas_call(
        finish, name="finish", out_shape=shapes, in_specs=[vmem] * 6, out_specs=[vmem] * 6
    )(*results)
    return (dq[None], dk[None], dv[None], hidden, route[0], dw[None])


def solution(mesh):
    in_specs = (
        P("dp", "ctx", "exp"),
        P("dp", "ctx", "exp"),
        P("dp", "ctx", "exp"),
        P("dp", "ctx", "exp"),
        P(),
        P(("ctx", "exp", "dp"), None),
        P(("ctx", "exp", "dp"), None),
        P(("ctx", "exp", "dp")),
        P(("ctx", "exp", "dp"), None),
        P("exp", ("ctx", "dp"), None),
    )
    out_specs = (
        P("dp", "ctx", "exp"),
        P("dp", "ctx", "exp"),
        P("dp", "ctx", "exp"),
        P(("ctx", "exp", "dp"), None),
        P(("ctx", "exp", "dp")),
        P("exp", ("ctx", "dp"), None),
    )
    return jax.shard_map(
        per_device, mesh=mesh, in_specs=in_specs, out_specs=out_specs, check_vma=False
    )
```
